128 devices in a mesh: ctx: 16 (over y, z_hi, core), head: 8 (over x, z_lo).
Axes of the slice: x: 4, y: 4, z: 4 (z_hi: 2, z_lo: 2; z = z_hi * 2 + z_lo), core: 2. Of those that a mesh axis runs over, the one named last changes fastest.
Arguments:
- queries: bfloat16 [2048, 64, 128], P('ctx', 'head'), may hold values from -16 to 16
- cache_keys: bfloat16 [131072, 8, 128], P('ctx', 'head'), may hold values from -16 to 16
- cache_values: bfloat16 [131072, 8, 128], P('ctx', 'head'), may hold values from -6 to 6
- new_keys: bfloat16 [2048, 8, 128], P('ctx', 'head'), may hold values from -16 to 16
- new_values: bfloat16 [2048, 8, 128], P('ctx', 'head'), may hold values from -6 to 6
- vertical_blocks: int32 [8, 256], P('head'), may hold values from 0 to 1023, as said below
- slash_offsets: int32 [8, 4], P('head'), may hold values from 16 to 271, as said below
- out_weight: bfloat16 [8192, 8192], P('head'), may hold values from -0.25 to 0.25
Outputs:
- mixed: bfloat16 [2048, 8192], P(('ctx', 'head'))
The draws below stay inside these ranges and needn't reach their ends.
Inputs may be any that keep to these rules, and one draw needn't show every extreme that they name: `vertical_blocks`: each row is ascending; its entry j lies in blocks 4 * j to 4 * j + 3, and its first entry is 0. `slash_offsets`: each row is ascending; its entry j lies in [16 + j * 64, 16 + (j + 1) * 64).
All inputs are finite; a program needn't handle non-finite values.
Results may differ from the reference program's by a relative error of at most 0.0051.
Values may be sent and summed in bfloat16 or wider, within the bound.
No kernel may reach another device: no remote copies, remote signals or barrier semaphores. Data moves between devices by JAX's collectives and lax.ppermute only.
A program may use at most 128 MiB of HBM per device.

```python
import jax
import jax.numpy as jnp
from jax import lax

D = 8192
H = 64
KVH = 8
DH = 128
BLK = 128
GROUP = 8
LB = 64
VPB = 16
NV = 256
NS = 4
TOKENS = 2048
CONTEXT = 131072
QB = 16
NB = 1024
N_CTX = 16


def draw_queries(key, part):
    key = jax.random.fold_in(key, 3)
    values = jnp.clip(1.7 * jax.random.normal(key, (TOKENS, H, DH), jnp.float32), -8.0, 8.0)
    return values.astype(jnp.bfloat16)


def draw_cache_keys(key, part):
    key = jax.random.fold_in(key, 5)
    values = jnp.clip(1.7 * jax.random.normal(key, (CONTEXT, KVH, DH), jnp.float32), -8.0, 8.0)
    return values.astype(jnp.bfloat16)


def draw_new_keys(key, part):
    key = jax.random.fold_in(key, 6)
    values = jnp.clip(1.7 * jax.random.normal(key, (TOKENS, KVH, DH), jnp.float32), -8.0, 8.0)
    return values.astype(jnp.bfloat16)


def draw_vertical_blocks(key, part):
    key = jax.random.fold_in(key, 7)
    jitter = jax.random.randint(key, (KVH, NV), 0, 4)
    column = jnp.arange(NV, dtype=jnp.int32)[None, :]
    return jnp.where(column == 0, 0, 4 * column + jitter).astype(jnp.int32)


def draw_slash_offsets(key, part):
    key = jax.random.fold_in(key, 9)
    first_key, second_key = jax.random.split(key)
    jitter = jax.random.randint(first_key, (KVH, NS), 0, LB)
    paired = jax.random.randint(second_key, (), 0, KVH)
    row_index = jnp.arange(KVH, dtype=jnp.int32)[:, None]
    column = jnp.arange(NS, dtype=jnp.int32)[None, :]
    jitter = jnp.where((row_index == paired) & (column == 0), LB - 1, jitter)
    jitter = jnp.where((row_index == paired) & (column == 1), 0, jitter)
    return (QB + column * LB + jitter).astype(jnp.int32)


def shard_levels(stream_key, extent, shards, least, high):
    gain, own = 1.0, jax.random.fold_in(stream_key, 6)
    for dim, shards_of in shards:
        heights = jnp.exp(jax.random.uniform(jax.random.fold_in(own, dim), (shards_of,), jnp.float32, least / len(shards), high / len(shards)))
        gain = gain * jnp.repeat(heights, extent[dim] // shards_of).reshape([-1 if axis == dim else 1 for axis in range(len(extent))])
    return gain


def scatter_about(stream_key, shape, scale, limit, shards=(), kind=jnp.bfloat16):
    drawn = scale * jax.random.normal(stream_key, shape, jnp.float32)
    if shards:
        drawn = drawn * shard_levels(stream_key, shape, shards, -0.22, 0.18)
    return jnp.clip(drawn, -limit, limit).astype(kind)


def setup_inputs(seed: int = 0) -> dict:
    key_list = jax.random.split(jax.random.key(seed), 9)
    queries = draw_queries(jax.random.fold_in(key_list[8], 71), 0)
    cache_keys = draw_cache_keys(jax.random.fold_in(key_list[8], 71), 0)
    cache_values = scatter_about(key_list[2], (CONTEXT, KVH, DH), 1.0, 6.0, ((0, 16), (1, 8)))
    new_keys = draw_new_keys(jax.random.fold_in(key_list[8], 71), 0)
    new_values = scatter_about(key_list[4], (TOKENS, KVH, DH), 1.0, 6.0, ((0, 16), (1, 8)))
    vertical_blocks = draw_vertical_blocks(jax.random.fold_in(key_list[8], 71), 0)
    slash_offsets = draw_slash_offsets(jax.random.fold_in(key_list[8], 71), 0)
    out_weight = scatter_about(key_list[7], (H * DH, D), (H * DH // 16) ** -0.5, 0.25, ((0, 8),))
    return {"queries": queries, "cache_keys": cache_keys, "cache_values": cache_values, "new_keys": new_keys, "new_values": new_values, "vertical_blocks": vertical_blocks, "slash_offsets": slash_offsets, "out_weight": out_weight}


NEGATIVE = -1e30


def reference(queries, cache_keys, cache_values, new_keys, new_values, vertical_blocks, slash_offsets, out_weight):
    score_scale = DH ** -0.5
    query_tiles = queries.reshape(QB, BLK, KVH, GROUP, DH)
    key_tiles = cache_keys.reshape(NB, BLK, KVH, DH)
    value_tiles = cache_values.reshape(NB, BLK, KVH, DH)
    fresh_keys = new_keys.reshape(QB, BLK, KVH, DH)
    fresh_values = new_values.reshape(QB, BLK, KVH, DH)
    causal = jnp.arange(BLK, dtype=jnp.int32)[:, None] >= jnp.arange(BLK, dtype=jnp.int32)[None, :]
    causal = jnp.repeat(causal, GROUP, axis=0)
    shard_ids = jnp.arange(N_CTX, dtype=jnp.int32)
    row_total = BLK * GROUP

    def per_head(kv_index):
        head_keys = lax.dynamic_index_in_dim(key_tiles, kv_index, 2, keepdims=False)
        head_values = lax.dynamic_index_in_dim(value_tiles, kv_index, 2, keepdims=False)
        vertical = lax.dynamic_index_in_dim(vertical_blocks, kv_index, 0, keepdims=False).astype(jnp.int32)
        offsets = lax.dynamic_index_in_dim(slash_offsets, kv_index, 0, keepdims=False).astype(jnp.int32)
        vert_keys = jnp.take(head_keys, vertical, axis=0).reshape(NV * BLK, DH)
        vert_values = jnp.take(head_values, vertical, axis=0).reshape(N_CTX, VPB * BLK, DH)
        last_repeated = jnp.any(vertical == NB - 1)

        def per_block(block_index):
            query_tile = lax.dynamic_index_in_dim(query_tiles, block_index, 0, keepdims=False)
            query_tile = lax.dynamic_index_in_dim(query_tile, kv_index, 1, keepdims=False).reshape(row_total, DH)
            slash_blocks = (NB + block_index - offsets).astype(jnp.int32)
            repeated = jnp.any(slash_blocks[:, None] == vertical[None, :], axis=1)
            owner_shard = (slash_blocks // LB).astype(jnp.int32)
            membership = owner_shard[:, None] == shard_ids[None, :]
            slash_keys = jnp.take(head_keys, slash_blocks, axis=0).reshape(NS * BLK, DH)
            slash_values = jnp.take(head_values, slash_blocks, axis=0)
            vert_scores = jnp.dot(query_tile, vert_keys.T, preferred_element_type=jnp.float32) * score_scale
            vert_scores = vert_scores.reshape(row_total, N_CTX, VPB * BLK)
            slash_scores = jnp.dot(query_tile, slash_keys.T, preferred_element_type=jnp.float32) * score_scale
            slash_scores = slash_scores.reshape(row_total, NS, BLK)
            slash_scores = jnp.where(repeated[None, :, None], NEGATIVE, slash_scores)
            slash_peak = jnp.max(slash_scores, axis=2)
            shard_slash = jnp.max(jnp.where(membership[None], slash_peak[:, :, None], NEGATIVE), axis=1)
            shard_peak = jnp.maximum(jnp.max(vert_scores, axis=2), shard_slash)
            vert_weights = jnp.exp(vert_scores - shard_peak[:, :, None])
            slash_reference = jnp.take(shard_peak, owner_shard, axis=1)
            slash_weights = jnp.exp(slash_scores - slash_reference[:, :, None])
            slash_sums = jnp.sum(slash_weights, axis=2)
            shard_sums = jnp.sum(vert_weights, axis=2) + jnp.sum(jnp.where(membership[None], slash_sums[:, :, None], 0.0), axis=1)
            vert_rounded = lax.optimization_barrier(vert_weights.astype(jnp.bfloat16)).astype(jnp.float32)
            slash_rounded = lax.optimization_barrier(slash_weights.astype(jnp.bfloat16)).astype(jnp.float32)
            vert_out = jnp.einsum("rnk,nkd->rnd", vert_rounded, vert_values.astype(jnp.float32))
            slash_out = jnp.einsum("rjk,jkd->rjd", slash_rounded, slash_values.astype(jnp.float32))
            shard_out = vert_out + jnp.sum(jnp.where(membership[None, :, :, None], slash_out[:, :, None, :], 0.0), axis=1)
            own_keys = lax.dynamic_index_in_dim(lax.dynamic_index_in_dim(fresh_keys, block_index, 0, keepdims=False), kv_index, 1, keepdims=False)
            own_values = lax.dynamic_index_in_dim(lax.dynamic_index_in_dim(fresh_values, block_index, 0, keepdims=False), kv_index, 1, keepdims=False)
            own_scores = jnp.dot(query_tile, own_keys.T, preferred_element_type=jnp.float32) * score_scale
            own_scores = jnp.where(causal, own_scores, NEGATIVE)
            own_peak = jnp.max(own_scores, axis=1)
            own_weights = jnp.exp(own_scores - own_peak[:, None])
            own_sum = jnp.sum(own_weights, axis=1)
            own_out = jnp.dot(own_weights.astype(jnp.bfloat16), own_values, preferred_element_type=jnp.float32)
            prior_index = jnp.maximum(block_index - 1, 0).astype(jnp.int32)
            prior_keys = lax.dynamic_index_in_dim(lax.dynamic_index_in_dim(fresh_keys, prior_index, 0, keepdims=False), kv_index, 1, keepdims=False)
            prior_values = lax.dynamic_index_in_dim(lax.dynamic_index_in_dim(fresh_values, prior_index, 0, keepdims=False), kv_index, 1, keepdims=False)
            near_keys = jnp.where(block_index > 0, prior_keys, head_keys[NB - 1])
            near_values = jnp.where(block_index > 0, prior_values, head_values[NB - 1])
            near_valid = jnp.logical_not((block_index == 0) & last_repeated)
            near_scores = jnp.dot(query_tile, near_keys.T, preferred_element_type=jnp.float32) * score_scale
            near_raw = jnp.max(near_scores, axis=1)
            near_weights = jnp.where(near_valid, jnp.exp(near_scores - near_raw[:, None]), 0.0)
            near_peak = jnp.where(near_valid, near_raw, NEGATIVE)
            near_sum = jnp.sum(near_weights, axis=1)
            near_out = jnp.dot(near_weights.astype(jnp.bfloat16), near_values, preferred_element_type=jnp.float32)
            global_peak = jnp.maximum(jnp.maximum(jnp.max(shard_peak, axis=1), own_peak), near_peak)
            shard_factor = jnp.exp(shard_peak - global_peak[:, None])
            own_factor = jnp.exp(own_peak - global_peak)
            near_factor = jnp.exp(near_peak - global_peak)
            weight_sum = jnp.sum(shard_sums * shard_factor, axis=1) + own_sum * own_factor + near_sum * near_factor
            blended = jnp.sum(shard_out * shard_factor[:, :, None], axis=1) + own_out * own_factor[:, None] + near_out * near_factor[:, None]
            return (blended / weight_sum[:, None]).astype(jnp.bfloat16)

        return lax.map(per_block, jnp.arange(QB, dtype=jnp.int32))

    attention = lax.map(per_head, jnp.arange(KVH, dtype=jnp.int32))
    attention = attention.reshape(KVH, QB, BLK, GROUP, DH)
    attention = jnp.transpose(attention, (1, 2, 0, 3, 4)).reshape(TOKENS, H * DH)
    return jnp.dot(attention, out_weight, preferred_element_type=jnp.float32).astype(jnp.bfloat16)
```

```python
import functools
import math

import jax
import jax.numpy as jnp
from jax import lax
from jax.experimental import pallas as pl
from jax.experimental.pallas import tpu as pltpu
from jax.sharding import PartitionSpec as P

BLK = 128
DH = 128
GROUP = 8
ROWS = BLK * GROUP
LB = 64
VPB = 16
NS = 4
NB = 1024
N_Y = 4
N_Z = 2
N_K = 2
N_X = 4
N_W = 2
QB = 16
PAR = QB // N_K
KEYS = VPB * BLK
STATS = 16
SCALE = DH**-0.5 * math.log2(math.e)
NEGATIVE = -1e30
LIMIT = 1e30
VMEM_BYTES = 30 * 2**20
LAST = (((1,), (1,)), ((), ()))


def ctx_shift(x, dy, dz, dk):
    pairs = []
    for y in range(N_Y):
        for z in range(N_Z):
            for k in range(N_K):
                source = (y * N_Z + z) * N_K + k
                target = (((y + dy) % N_Y) * N_Z + (z + dz) % N_Z) * N_K + (k + dk) % N_K
                pairs.append((source, target))
    return lax.ppermute(x, "ctx", pairs)


def head_shift(array, dx, dw):
    pairs = []
    for x in range(N_X):
        for w in range(N_W):
            pairs.append((x * N_W + w, ((x + dx) % N_X) * N_W + (w + dw) % N_W))
    return lax.ppermute(array, "head", pairs)


def gather_kernel(
    info_ref, vert_ref, offs_ref, keys_ref, values_ref, kv_ref, mine_ref, away_ref, staged, sems
):
    shard = info_ref[0]
    parity = info_ref[1]
    first = shard * LB

    def copies(block, out_ref, index, half, stage, number):
        start = pl.multiple_of(block * BLK, BLK)
        return (
            pltpu.make_async_copy(
                keys_ref.at[pl.ds(start, BLK)],
                out_ref.at[pl.ds(index * BLK, BLK)],
                sems.at[2 * number],
            ),
            pltpu.make_async_copy(
                values_ref.at[pl.ds(start, BLK)], staged.at[stage], sems.at[2 * number + 1]
            ),
        )

    def vertical(i):
        block = vert_ref[0, shard * VPB + i] - first
        return copies(block, kv_ref, i, VPB, i, i)

    def slash(out_ref, base, query_block, n):
        bi, slot = n // 2, n % 2
        b = 2 * bi + query_block
        lower = NB + b - offs_ref[0, slot]
        upper = NB + b - offs_ref[0, slot + 2]
        lower_in = (lower >> 6) == shard
        block = jnp.where(lower_in, lower, upper)
        usable = ((block >> 6) == shard) & (vert_ref[0, block >> 2] != block)
        return usable, copies(block & (LB - 1), out_ref, n, 2 * PAR, base + n, base + n)

    sets = ((mine_ref, VPB, parity), (away_ref, VPB + 2 * PAR, 1 - parity))
    for i in range(VPB):
        for copy in vertical(i):
            copy.start()
    for out_ref, base, query_block in sets:
        for n in range(2 * PAR):
            usable, pair = slash(out_ref, base, query_block, n)

            @pl.when(usable)
            def _(pair=pair):
                for copy in pair:
                    copy.start()

    for i in range(VPB):
        for copy in vertical(i):
            copy.wait()
        kv_ref[KEYS + i * BLK : KEYS + (i + 1) * BLK, :] = staged[i].T
    for out_ref, base, query_block in sets:
        for n in range(2 * PAR):
            usable, pair = slash(out_ref, base, query_block, n)

            @pl.when(usable)
            def _(pair=pair, out_ref=out_ref, n=n, base=base):
                for copy in pair:
                    copy.wait()
                at = 2 * PAR * BLK + n * BLK
                out_ref[at : at + BLK, :] = staged[base + n].T


def gather_blocks(info, vertical_blocks, slash_offsets, keys, values):
    whole = pl.BlockSpec(memory_space=pltpu.VMEM)
    smem = pl.BlockSpec(memory_space=pltpu.SMEM)
    anywhere = pl.BlockSpec(memory_space=pl.ANY)
    return pl.pallas_call(
        gather_kernel,
        out_shape=[
            jax.ShapeDtypeStruct((2 * KEYS, DH), jnp.bfloat16),
            jax.ShapeDtypeStruct((4 * PAR * BLK, DH), jnp.bfloat16),
            jax.ShapeDtypeStruct((4 * PAR * BLK, DH), jnp.bfloat16),
        ],
        in_specs=[smem, smem, smem, anywhere, anywhere],
        out_specs=[whole, whole, whole],
        scratch_shapes=[
            pltpu.VMEM((VPB + 4 * PAR, BLK, DH), jnp.bfloat16),
            pltpu.SemaphoreType.DMA((2 * (VPB + 4 * PAR),)),
        ],
        compiler_params=pltpu.CompilerParams(vmem_limit_bytes=16 * 2**20),
        cost_estimate=pl.CostEstimate(flops=0, bytes_accessed=8 * 2**20, transcendentals=0),
        name="gather_blocks",
    )(info, vertical_blocks, slash_offsets, keys, values)


def attend_kernel(has_state, is_home, *refs):
    info_ref, vert_ref, offs_ref, q_ref, own_ref, peer_ref, mine_ref, theirs_ref = refs[:8]
    refs = refs[8:]
    if has_state:
        state_ref, refs = refs[0], refs[1:]
    if is_home:
        fresh_ref, near_ref, refs = refs[0], refs[1], refs[2:]
    out_ref, total, peak, weight = refs
    rows = q_ref.shape[0]
    shard = info_ref[0]
    query_block = info_ref[2]

    def scores(keys):
        return lax.dot_general(keys, q_ref[...], LAST, preferred_element_type=jnp.float32) * SCALE

    def begin():
        if has_state:
            total[...] = state_ref[:DH, :].astype(jnp.float32)
            stats = state_ref[DH:, :].astype(jnp.float32)
            peak[0:1, :] = stats[0:1] + stats[1:2] + stats[2:3]
            weight[0:1, :] = jnp.ones((1, rows), jnp.float32)
        else:
            total[...] = jnp.zeros_like(total)
            peak[0:1, :] = jnp.max(scores(own_ref[:BLK, :]), axis=0, keepdims=True)
            weight[0:1, :] = jnp.zeros((1, rows), jnp.float32)

    def careful(keys, values, allowed=None):
        s = scores(keys)
        if allowed is not None:
            s = jnp.where(allowed, s, NEGATIVE)
        before = peak[0:1, :]
        now = jnp.maximum(before, jnp.max(s, axis=0, keepdims=True))
        shrink = jnp.exp2(before - now)
        p = jnp.exp2(s - now)
        weight[0:1, :] = weight[0:1, :] * shrink + jnp.sum(p, axis=0, keepdims=True)
        total[...] = total[...] * shrink + jnp.dot(
            values, p.astype(jnp.bfloat16), preferred_element_type=jnp.float32
        )
        peak[0:1, :] = now

    begin()
    for ref in (own_ref, peer_ref):
        values = jnp.concatenate(
            [ref[KEYS + i * BLK : KEYS + (i + 1) * BLK, :] for i in range(VPB)], axis=1
        )
        p = jnp.exp2(scores(ref[:KEYS, :]) - peak[0:1, :])
        weight[0:1, :] += jnp.sum(p, axis=0, keepdims=True)
        total[...] += jnp.dot(values, p.astype(jnp.bfloat16), preferred_element_type=jnp.float32)
    outside = jnp.max(jnp.where(weight[0:1, :] < LIMIT, 0.0, 1.0))

    @pl.when(outside > 0.0)
    def _():
        begin()
        for ref in (own_ref, peer_ref):

            def step(i, carry, ref=ref):
                at = pl.multiple_of(i * BLK, BLK)
                careful(ref[pl.ds(at, BLK), :], ref[pl.ds(KEYS + at, BLK), :])
                return carry

            lax.fori_loop(0, VPB, step, 0)

    for j in range(NS):
        block = NB + query_block - offs_ref[0, j]
        fresh = vert_ref[0, block >> 2] != block
        at = pl.multiple_of(((query_block // 2) * 2 + j % 2) * BLK, BLK)
        for ref, holder in ((mine_ref, shard), (theirs_ref, shard ^ 1)):

            @pl.when(fresh & ((block >> 6) == holder))
            def _(ref=ref, at=at):
                careful(ref[pl.ds(at, BLK), :], ref[pl.ds(2 * PAR * BLK + at, BLK), :])

    if is_home:
        key_at = lax.broadcasted_iota(jnp.int32, (BLK, rows), 0)
        token = lax.broadcasted_iota(jnp.int32, (BLK, rows), 1) % BLK
        careful(fresh_ref[:BLK, :], fresh_ref[BLK:, :], key_at <= token)
        last_repeated = vert_ref[0, NB // 4 - 1] == NB - 1

        @pl.when(jnp.logical_not((query_block == 0) & last_repeated))
        def _():
            careful(near_ref[:BLK, :], near_ref[BLK:, :])

    weights = weight[0:1, :]
    result = total[...] * (1.0 / weights)
    level = peak[0:1, :] + jnp.log2(weights)
    if is_home:
        out_ref[:DH, :] = result
        out_ref[DH:, :] = jnp.broadcast_to(level, (8, rows))
    else:
        out_ref[:DH, :] = result.astype(jnp.bfloat16)
        high = level.astype(jnp.bfloat16).astype(jnp.float32)
        middle = (level - high).astype(jnp.bfloat16).astype(jnp.float32)
        low = level - high - middle
        line = lax.broadcasted_iota(jnp.int32, (STATS, rows), 0)
        stats = jnp.where(line == 0, high, jnp.where(line == 1, middle, jnp.where(line == 2, low, 0.0)))
        out_ref[DH:, :] = stats.astype(jnp.bfloat16)


def attend(info, vertical_blocks, slash_offsets, q, blocks, state=None, home=None, name="attend"):
    rows = q.shape[0]
    whole = pl.BlockSpec(memory_space=pltpu.VMEM)
    smem = pl.BlockSpec(memory_space=pltpu.SMEM)
    operands = [info, vertical_blocks, slash_offsets, q, *blocks]
    specs = [smem] * 3 + [whole] * 5
    if state is not None:
        operands.append(state)
        specs.append(whole)
    if home is not None:
        operands.extend(home)
        specs.extend([whole, whole])
        shape = jax.ShapeDtypeStruct((DH + 8, rows), jnp.float32)
    else:
        shape = jax.ShapeDtypeStruct((DH + STATS, rows), jnp.bfloat16)
    scored = 2 * KEYS * rows
    return pl.pallas_call(
        functools.partial(attend_kernel, state is not None, home is not None),
        out_shape=shape,
        in_specs=specs,
        out_specs=whole,
        scratch_shapes=[
            pltpu.VMEM((DH, rows), jnp.float32),
            pltpu.VMEM((8, rows), jnp.float32),
            pltpu.VMEM((8, rows), jnp.float32),
        ],
        compiler_params=pltpu.CompilerParams(vmem_limit_bytes=VMEM_BYTES),
        cost_estimate=pl.CostEstimate(
            flops=scored * DH * 4, bytes_accessed=4 * 2**20, transcendentals=scored
        ),
        name=name,
    )(*operands)


def merge_kernel(home_ref, *refs):
    part_refs, out_ref = refs[:-1], refs[-1]
    levels = [home_ref[DH : DH + 1, :]]
    for ref in part_refs:
        stats = ref[DH:, :].astype(jnp.float32)
        levels.append(stats[0:1] + stats[1:2] + stats[2:3])
    highest = functools.reduce(jnp.maximum, levels)
    factors = [jnp.exp2(level - highest) for level in levels]
    blended = home_ref[:DH, :] * factors[0]
    for ref, factor in zip(part_refs, factors[1:]):
        blended += ref[:DH, :].astype(jnp.float32) * factor
    blended = blended * (1.0 / sum(factors))
    for h in range(GROUP):
        out_ref[:, h * DH : (h + 1) * DH] = (
            blended[:, h * BLK : (h + 1) * BLK].T.astype(jnp.bfloat16)
        )


def merge(home, parts):
    whole = pl.BlockSpec(memory_space=pltpu.VMEM)
    return pl.pallas_call(
        merge_kernel,
        out_shape=jax.ShapeDtypeStruct((BLK, GROUP * DH), jnp.bfloat16),
        in_specs=[whole] * (1 + len(parts)),
        out_specs=whole,
        compiler_params=pltpu.CompilerParams(vmem_limit_bytes=16 * 2**20),
        cost_estimate=pl.CostEstimate(
            flops=8 * ROWS * DH, bytes_accessed=2 * 2**20, transcendentals=4 * ROWS
        ),
        name="merge",
    )(home, *parts)


def local(
    queries,
    cache_keys,
    cache_values,
    new_keys,
    new_values,
    vertical_blocks,
    slash_offsets,
    out_weight,
):
    index = lax.axis_index("ctx")
    parity = index % 2
    column = index % (N_Z * N_K)
    cross = column ^ N_K
    y = index // (N_Z * N_K)

    def info(query_block):
        return jnp.stack([index, parity, query_block, 0]).astype(jnp.int32)

    keys = cache_keys.reshape(-1, DH)
    values = cache_values.reshape(-1, DH)
    q = jnp.transpose(queries, (1, 0, 2)).reshape(ROWS, DH)
    q_cross = ctx_shift(q, 0, 1, 0)
    kv, mine, away = gather_blocks(info(index), vertical_blocks, slash_offsets, keys, values)
    peer = ctx_shift(kv, 0, 0, 1)
    theirs = ctx_shift(away, 0, 0, 1)
    blocks = (kv, peer, mine, theirs)

    fresh = jnp.concatenate([new_keys.reshape(BLK, DH), new_values.reshape(BLK, DH).T], axis=0)
    final = jnp.concatenate([keys[-BLK:], values[-BLK:].T], axis=0)
    sent = jnp.where(index == 15, final, fresh)
    near = lax.ppermute(sent, "ctx", [(i, (i + 1) % 16) for i in range(16)])

    shifts = (1, 3, 2)
    q_far_cross = [ctx_shift(q_cross, dy, 0, 0) for dy in shifts]
    q_far = [ctx_shift(q, dy, 0, 0) for dy in shifts]

    def block_of(dy, where):
        return ((y - dy) % N_Y) * (N_Z * N_K) + where

    home = attend(
        info(index), vertical_blocks, slash_offsets, q, blocks, home=(fresh, near), name="home"
    )
    states = []
    for dy, rows in zip((0,) + shifts, [q_cross] + q_far_cross):
        part = attend(
            info(block_of(dy, cross)), vertical_blocks, slash_offsets, rows, blocks, name=f"far_{dy}"
        )
        states.append(ctx_shift(part, 0, 1, 0))
    parts = []
    for dy, rows, state in zip(shifts, q_far, states[1:]):
        part = attend(
            info(block_of(dy, column)),
            vertical_blocks,
            slash_offsets,
            rows,
            blocks,
            state=state,
            name=f"near_{dy}",
        )
        parts.append(ctx_shift(part, -dy, 0, 0))
    attention = merge(home, [states[0], *parts])
    partial = jnp.dot(attention, out_weight, preferred_element_type=jnp.float32)
    partial = partial.astype(jnp.bfloat16).reshape(N_X * N_W, BLK // (N_X * N_W), -1)
    place = lax.axis_index("head")
    x, w = place // N_W, place % N_W
    summed = lax.dynamic_index_in_dim(partial, place, 0, keepdims=False).astype(jnp.float32)
    received = []
    for dx in range(N_X):
        for dw in range(N_W):
            if dx or dw:
                target = ((x + dx) % N_X) * N_W + (w + dw) % N_W
                piece = lax.dynamic_index_in_dim(partial, target, 0, keepdims=False)
                received.append(head_shift(piece, dx, dw))
    for piece in received:
        summed = summed + piece.astype(jnp.float32)
    return summed.astype(jnp.bfloat16)


def solution(mesh):
    in_specs = (
        P("ctx", "head", None),
        P("ctx", "head", None),
        P("ctx", "head", None),
        P("ctx", "head", None),
        P("ctx", "head", None),
        P("head", None),
        P("head", None),
        P("head", None),
    )
    out_specs = P(("ctx", "head"), None)
    return jax.shard_map(local, mesh=mesh, in_specs=in_specs, out_specs=out_specs, check_vma=False)
```

```python
import functools
import math

import jax
import jax.numpy as jnp
from jax import lax
from jax.experimental import pallas as pl
from jax.experimental.pallas import tpu as pltpu
from jax.sharding import PartitionSpec as P

BLK = 128
DH = 128
GROUP = 8
ROWS = BLK * GROUP
LB = 64
VPB = 16
NS = 4
NB = 1024
N_Y = 4
N_Z = 2
N_K = 2
N_X = 4
N_W = 2
QB = 16
PAR = QB // N_K
KEYS = VPB * BLK
STATS = 16
SLOTS = 2 * PAR
SLASH_REACH = 271
OFFSETS = 4
VERTICAL = 8
HEADS = N_X * N_W
SHARE = BLK // HEADS
TILE = 1024
SCALE = DH**-0.5 * math.log2(math.e)
NEGATIVE = -1e30
LIMIT = 1e30
VMEM_BYTES = 24 * 2**20
LAST = (((1,), (1,)), ((), ()))


def ctx_shift(x, dy, dz, dk):
    pairs = []
    for y in range(N_Y):
        for z in range(N_Z):
            for k in range(N_K):
                source = (y * N_Z + z) * N_K + k
                target = (((y + dy) % N_Y) * N_Z + (z + dz) % N_Z) * N_K + (k + dk) % N_K
                pairs.append((source, target))
    return lax.ppermute(x, "ctx", pairs)


def head_shift(array, dx, dw):
    pairs = []
    for x in range(N_X):
        for w in range(N_W):
            pairs.append((x * N_W + w, ((x + dx) % N_X) * N_W + (w + dw) % N_W))
    return lax.ppermute(array, "head", pairs)


def gather_kernel(
    info_ref,
    keys_ref,
    values_ref,
    fresh_keys_ref,
    fresh_values_ref,
    kv_ref,
    away_ref,
    next_ref,
    staged,
    sems,
    slash_sems,
    next_sems,
):
    shard = info_ref[0]
    away = 1 - info_ref[1]
    first = shard * LB

    def rows(block):
        return pl.ds(pl.multiple_of(block * BLK, BLK), BLK)

    def vertical(i):
        block = info_ref[VERTICAL + shard * VPB + i] - first
        return (
            pltpu.make_async_copy(
                values_ref.at[rows(block)], staged.at[i], sems.at[2 * i]
            ),
            pltpu.make_async_copy(
                keys_ref.at[rows(block)], kv_ref.at[pl.ds(i * BLK, BLK)], sems.at[2 * i + 1]
            ),
        )

    def slash(n):
        lower, upper = (
            NB + 2 * (n // 2) + away - info_ref[OFFSETS + n % 2 + late] for late in (0, 2)
        )
        block = jnp.where((lower >> 6) == shard, lower, upper)
        usable = ((block >> 6) == shard) & (info_ref[VERTICAL + (block >> 2)] != block)
        local_rows = rows(block & (LB - 1))
        pair = (
            pltpu.make_async_copy(
                keys_ref.at[local_rows], away_ref.at[pl.ds(n * BLK, BLK)], slash_sems.at[2 * n]
            ),
            pltpu.make_async_copy(
                values_ref.at[local_rows],
                away_ref.at[pl.ds((SLOTS + n) * BLK, BLK)],
                slash_sems.at[2 * n + 1],
            ),
        )
        return usable, pair

    def following(keys, values):
        return (
            pltpu.make_async_copy(keys, next_ref.at[pl.ds(0, BLK)], next_sems.at[0]),
            pltpu.make_async_copy(values, next_ref.at[pl.ds(BLK, BLK)], next_sems.at[1]),
        )

    tail = pl.ds((LB - 1) * BLK, BLK)
    last = shard == N_Y * N_Z * N_K - 1
    from_cache = following(keys_ref.at[tail], values_ref.at[tail])
    from_fresh = following(fresh_keys_ref, fresh_values_ref)

    for i in range(VPB):
        for copy in vertical(i):
            copy.start()

    @pl.when(last)
    def _():
        for copy in from_cache:
            copy.start()

    @pl.when(jnp.logical_not(last))
    def _():
        for copy in from_fresh:
            copy.start()

    holds_slash = (shard + 1) * LB > NB - SLASH_REACH

    @pl.when(holds_slash)
    def _():
        for n in range(SLOTS):
            usable, pair = slash(n)

            @pl.when(usable)
            def _(pair=pair):
                for copy in pair:
                    copy.start()

    for i in range(VPB):
        for copy in vertical(i):
            copy.wait()
        kv_ref[KEYS + i * BLK : KEYS + (i + 1) * BLK, :] = staged[i].T

    @pl.when(holds_slash)
    def _():
        for n in range(SLOTS):
            usable, pair = slash(n)

            @pl.when(usable)
            def _(pair=pair):
                for copy in pair:
                    copy.wait()

    @pl.when(last)
    def _():
        for copy in from_cache:
            copy.wait()

    @pl.when(jnp.logical_not(last))
    def _():
        for copy in from_fresh:
            copy.wait()


WHOLE = pl.BlockSpec(memory_space=pltpu.VMEM)
SCALARS = pl.BlockSpec(memory_space=pltpu.SMEM)
IN_HBM = pl.BlockSpec(memory_space=pltpu.HBM)


def gather_blocks(info, keys, values, fresh_keys, fresh_values):
    return pl.pallas_call(
        gather_kernel,
        out_shape=[
            jax.ShapeDtypeStruct((2 * KEYS, DH), jnp.bfloat16),
            jax.ShapeDtypeStruct((2 * SLOTS * BLK, DH), jnp.bfloat16),
            jax.ShapeDtypeStruct((2 * BLK, DH), jnp.bfloat16),
        ],
        in_specs=[SCALARS, IN_HBM, IN_HBM, IN_HBM, IN_HBM],
        out_specs=[WHOLE, IN_HBM, IN_HBM],
        scratch_shapes=[
            pltpu.VMEM((VPB, BLK, DH), jnp.bfloat16),
            pltpu.SemaphoreType.DMA((2 * VPB,)),
            pltpu.SemaphoreType.DMA((2 * SLOTS,)),
            pltpu.SemaphoreType.DMA((2,)),
        ],
        compiler_params=pltpu.CompilerParams(vmem_limit_bytes=8 * 2**20),
        cost_estimate=pl.CostEstimate(flops=0, bytes_accessed=12 * 2**20, transcendentals=0),
        name="gather_blocks",
    )(info, keys, values, fresh_keys, fresh_values)


def attend_kernel(is_home, *refs):
    info_ref, q_ref, own_ref, peer_ref, keys_ref, values_ref, theirs_ref = refs[:7]
    refs = refs[7:]
    if is_home:
        (fresh_keys_ref, fresh_values_ref, near_ref), refs = refs[:3], refs[3:]
    out_ref, total, peak, weight, slash_keys, slash_values, sems = refs
    rows = q_ref.shape[0]
    shard = info_ref[0]
    query_block = info_ref[2]

    def slash(j):
        block = NB + query_block - info_ref[OFFSETS + j]
        fresh = info_ref[VERTICAL + (block >> 2)] != block
        slot = (query_block >> 1) * 2 + j % 2
        local_at = pl.multiple_of((block & (LB - 1)) * BLK, BLK)
        their_at = pl.multiple_of(slot * BLK, BLK)

        def pair(own):
            if own:
                sources = keys_ref.at[pl.ds(local_at, BLK)], values_ref.at[pl.ds(local_at, BLK)]
            else:
                sources = (
                    theirs_ref.at[pl.ds(their_at, BLK)],
                    theirs_ref.at[pl.ds(SLOTS * BLK + their_at, BLK)],
                )
            return (
                pltpu.make_async_copy(sources[0], slash_keys.at[j], sems.at[2 * j]),
                pltpu.make_async_copy(sources[1], slash_values.at[j], sems.at[2 * j + 1]),
            )

        holder = block >> 6
        return fresh & (holder == shard), fresh & (holder == (shard ^ 1)), pair

    for j in range(NS):
        is_mine, is_theirs, pair = slash(j)
        for own, held in ((True, is_mine), (False, is_theirs)):

            @pl.when(held)
            def _(pair=pair, own=own):
                for copy in pair(own):
                    copy.start()

    def scores(keys):
        return lax.dot_general(keys, q_ref[...], LAST, preferred_element_type=jnp.float32) * SCALE

    def weigh(values, p):
        width = values.shape[1]
        marked = jnp.concatenate([values, jnp.ones((STATS, width), jnp.bfloat16)], axis=0)
        return jnp.dot(marked, p.astype(jnp.bfloat16), preferred_element_type=jnp.float32)

    def begin():
        total[...] = jnp.zeros_like(total)
        peak[0:1, :] = jnp.max(scores(own_ref[:BLK, :]), axis=0, keepdims=True)
        weight[0:1, :] = jnp.zeros((1, rows), jnp.float32)

    def careful(keys, values, allowed=None):
        s = scores(keys)
        if allowed is not None:
            s = jnp.where(allowed, s, NEGATIVE)
        before = peak[0:1, :]
        now = jnp.maximum(before, jnp.max(s, axis=0, keepdims=True))
        shrink = jnp.exp2(before - now)
        added = weigh(values, jnp.exp2(s - now))
        weight[0:1, :] = weight[0:1, :] * shrink + added[DH : DH + 1]
        total[...] = total[...] * shrink + added[:DH]
        peak[0:1, :] = now

    begin()
    for ref in (own_ref, peer_ref):
        values = jnp.concatenate(
            [ref[KEYS + i * BLK : KEYS + (i + 1) * BLK, :] for i in range(VPB)], axis=1
        )
        added = weigh(values, jnp.exp2(scores(ref[:KEYS, :]) - peak[0:1, :]))
        weight[0:1, :] += added[DH : DH + 1]
        total[...] += added[:DH]
    outside = jnp.max(jnp.where(weight[0:1, :] < LIMIT, 0.0, 1.0))

    @pl.when(outside > 0.0)
    def _():
        begin()
        for ref in (own_ref, peer_ref):

            def step(i, carry, ref=ref):
                at = pl.multiple_of(i * BLK, BLK)
                careful(ref[pl.ds(at, BLK), :], ref[pl.ds(KEYS + at, BLK), :])
                return carry

            lax.fori_loop(0, VPB, step, 0)

    for j in range(NS):
        is_mine, is_theirs, pair = slash(j)

        @pl.when(is_mine | is_theirs)
        def _(j=j, pair=pair):
            for copy in pair(True):
                copy.wait()
            careful(slash_keys[j], slash_values[j].T)

    if is_home:
        key_at = lax.broadcasted_iota(jnp.int32, (BLK, rows), 0)
        token = lax.broadcasted_iota(jnp.int32, (BLK, rows), 1) % BLK
        careful(fresh_keys_ref[...], fresh_values_ref[...].T, key_at <= token)
        last_repeated = info_ref[VERTICAL + NB // 4 - 1] == NB - 1

        @pl.when(jnp.logical_not((query_block == 0) & last_repeated))
        def _():
            careful(near_ref[:BLK, :], near_ref[BLK:, :].T)

    weights = weight[0:1, :]
    result = total[...] * (1.0 / weights)
    level = peak[0:1, :] + jnp.log2(weights)
    if is_home:
        out_ref[:DH, :] = result
        out_ref[DH:, :] = jnp.broadcast_to(level, (8, rows))
    else:
        out_ref[:DH, :] = result.astype(jnp.bfloat16)
        high = level.astype(jnp.bfloat16).astype(jnp.float32)
        middle = (level - high).astype(jnp.bfloat16).astype(jnp.float32)
        low = level - high - middle
        line = lax.broadcasted_iota(jnp.int32, (STATS, rows), 0)
        stats = jnp.where(line == 0, high, jnp.where(line == 1, middle, jnp.where(line == 2, low, 0.0)))
        out_ref[DH:, :] = stats.astype(jnp.bfloat16)


def attend(info, q, blocks, home=(), name="attend"):
    rows = q.shape[0]
    if home:
        shape = jax.ShapeDtypeStruct((DH + 8, rows), jnp.float32)
    else:
        shape = jax.ShapeDtypeStruct((DH + STATS, rows), jnp.bfloat16)
    scored = 2 * KEYS * rows
    return pl.pallas_call(
        functools.partial(attend_kernel, bool(home)),
        out_shape=shape,
        in_specs=[SCALARS] + [WHOLE] * 3 + [IN_HBM] * 3 + [WHOLE] * len(home),
        out_specs=WHOLE,
        scratch_shapes=[
            pltpu.VMEM((DH, rows), jnp.float32),
            pltpu.VMEM((8, rows), jnp.float32),
            pltpu.VMEM((8, rows), jnp.float32),
            pltpu.VMEM((NS, BLK, DH), jnp.bfloat16),
            pltpu.VMEM((NS, BLK, DH), jnp.bfloat16),
            pltpu.SemaphoreType.DMA((2 * NS,)),
        ],
        compiler_params=pltpu.CompilerParams(vmem_limit_bytes=VMEM_BYTES),
        cost_estimate=pl.CostEstimate(
            flops=scored * DH * 4, bytes_accessed=4 * 2**20, transcendentals=scored
        ),
        name=name,
    )(info, q, *blocks, *home)


def project_kernel(info_ref, home_ref, *refs):
    count = N_Y * N_Z - 1
    part_refs, weight_ref = refs[:count], refs[count]
    out_refs, (natural, rotated) = refs[count + 1 : -2], refs[-2:]
    levels = [home_ref[DH : DH + 1, :]]
    for ref in part_refs:
        stats = ref[DH:, :].astype(jnp.float32)
        levels.append(stats[0:1] + stats[1:2] + stats[2:3])
    highest = functools.reduce(jnp.maximum, levels)
    factors = [jnp.exp2(level - highest) for level in levels]
    blended = home_ref[:DH, :] * factors[0]
    for ref, factor in zip(part_refs, factors[1:]):
        blended += ref[:DH, :].astype(jnp.float32) * factor
    blended = blended * (1.0 / sum(factors))
    for h in range(GROUP):
        natural[:, h * DH : (h + 1) * DH] = (
            blended[:, h * BLK : (h + 1) * BLK].T.astype(jnp.bfloat16)
        )
    place = info_ref[3]
    x, w = place >> 1, place & 1
    for at in range(HEADS):
        target = ((x + at // N_W) & (N_X - 1)) * N_W + ((w + at) & 1)
        rotated[at * SHARE : (at + 1) * SHARE, :] = natural[
            pl.ds(pl.multiple_of(target * SHARE, SHARE), SHARE), :
        ]
    for column in range(0, weight_ref.shape[1], TILE):
        partial = jnp.dot(
            rotated[...],
            weight_ref[:, column : column + TILE],
            preferred_element_type=jnp.float32,
        ).astype(jnp.bfloat16)
        for at in range(HEADS):
            out_refs[at][:, column : column + TILE] = partial[at * SHARE : (at + 1) * SHARE, :]


def project(info, home, parts, out_weight):
    depth, width = out_weight.shape
    return pl.pallas_call(
        project_kernel,
        out_shape=[jax.ShapeDtypeStruct((SHARE, width), jnp.bfloat16)] * HEADS,
        in_specs=[SCALARS] + [WHOLE] * (2 + len(parts)),
        out_specs=[WHOLE] * HEADS,
        scratch_shapes=[
            pltpu.VMEM((BLK, depth), jnp.bfloat16),
            pltpu.VMEM((BLK, depth), jnp.bfloat16),
        ],
        compiler_params=pltpu.CompilerParams(vmem_limit_bytes=12 * 2**20),
        cost_estimate=pl.CostEstimate(
            flops=2 * BLK * depth * width, bytes_accessed=2 * depth * width, transcendentals=0
        ),
        name="project",
    )(info, home, *parts, in_vmem(out_weight))


def in_hbm(x):
    return pltpu.with_memory_space_constraint(x, pltpu.HBM)


def in_vmem(x):
    return pltpu.with_memory_space_constraint(x, pltpu.VMEM)


def after(x, *earlier):
    return lax.optimization_barrier((x, *earlier))[0]


def local(
    queries,
    cache_keys,
    cache_values,
    new_keys,
    new_values,
    vertical_blocks,
    slash_offsets,
    out_weight,
):
    index = lax.axis_index("ctx")
    place = lax.axis_index("head")
    column = index % (N_Z * N_K)
    y = index // (N_Z * N_K)

    def info(dy=0, dz=0):
        query_block = ((y - dy) % N_Y) * (N_Z * N_K) + (column ^ (N_K * dz))
        head = jnp.stack([index, index % N_K, query_block, place]).astype(jnp.int32)
        return jnp.concatenate([head, slash_offsets[0], vertical_blocks[0]])

    keys = in_hbm(cache_keys.reshape(-1, DH))
    values = in_hbm(cache_values.reshape(-1, DH))
    fresh_keys = new_keys.reshape(BLK, DH)
    fresh_values = new_values.reshape(BLK, DH)
    q = jnp.transpose(queries, (1, 0, 2)).reshape(ROWS, DH)
    held = {(0, 0): q, (0, 1): ctx_shift(q, 0, 1, 0)}
    for dy in (1, 3):
        held[dy, 0] = ctx_shift(q, dy, 0, 0)
    kv, away, following = gather_blocks(
        info(), keys, values, in_hbm(fresh_keys), in_hbm(fresh_values)
    )
    peer = ctx_shift(kv, 0, 0, 1)
    theirs = ctx_shift(away, 0, 0, 1)
    near = lax.ppermute(following, "ctx", [(i, (i + 1) % 16) for i in range(16)])
    for dy in (1, 3):
        held[dy, 1] = ctx_shift(held[0, 1], dy, 0, 0)

    blocks = (in_vmem(kv), in_vmem(peer), keys, values, in_hbm(theirs))
    parts = []
    part = None
    for dy, dz in ((1, 0), (3, 0), (1, 1), (3, 1), (2, 0), (2, 1), (0, 1)):
        if part is None:
            rows = held[dy, dz]
        else:
            if len(parts) == 1:
                for z in range(N_Z):
                    held[2, z] = ctx_shift(after(held[0, z], part), 2, 0, 0)
            rows = after(held[dy, dz], part)
        part = attend(info(dy, dz), in_vmem(rows), blocks, name=f"attend_{dy}{dz}")
        parts.append(ctx_shift(part, -dy, dz, 0))
    home = attend(
        info(), in_vmem(after(q, part)), blocks, home=(fresh_keys, fresh_values, near), name="home"
    )
    pieces = project(info(), home, parts, out_weight)
    summed = pieces[0].astype(jnp.float32)
    received = []
    for at in range(1, HEADS):
        received.append(head_shift(pieces[at], at // N_W, at % N_W))
    for piece in received:
        summed = summed + piece.astype(jnp.float32)
    return summed.astype(jnp.bfloat16)


def solution(mesh):
    in_specs = (
        P("ctx", "head", None),
        P("ctx", "head", None),
        P("ctx", "head", None),
        P("ctx", "head", None),
        P("ctx", "head", None),
        P("head", None),
        P("head", None),
        P("head", None),
    )
    out_specs = P(("ctx", "head"), None)
    return jax.shard_map(local, mesh=mesh, in_specs=in_specs, out_specs=out_specs, check_vma=False)
```

```python
import functools
import math

import jax
import jax.numpy as jnp
from jax import lax
from jax.experimental import pallas as pl
from jax.experimental.pallas import tpu as pltpu
from jax.sharding import PartitionSpec as P

BLK = 128
DH = 128
GROUP = 8
ROWS = BLK * GROUP
LB = 64
VPB = 16
NS = 4
NB = 1024
N_Y = 4
N_Z = 2
N_K = 2
N_X = 4
N_W = 2
QB = 16
PAR = QB // N_K
KEYS = VPB * BLK
STATS = 16
SLOTS = 2 * PAR
SLASH_REACH = 271
NV = NB // 4
HEADS = N_X * N_W
SHARE = BLK // HEADS
TILE = 1024
LAG = 3
FAR = "far"
FIRST = "home_first"
LAST_HALF = "home_last"
PLACES = 3
SCALE = DH**-0.5 * math.log2(math.e)
NEGATIVE = -1e30
LIMIT = 1e30
VMEM_BYTES = 24 * 2**20
LAST = (((1,), (1,)), ((), ()))


def ctx_shift(x, dy, dz, dk):
    pairs = []
    for y in range(N_Y):
        for z in range(N_Z):
            for k in range(N_K):
                source = (y * N_Z + z) * N_K + k
                target = (((y + dy) % N_Y) * N_Z + (z + dz) % N_Z) * N_K + (k + dk) % N_K
                pairs.append((source, target))
    return lax.ppermute(x, "ctx", pairs)


def head_shift(array, dx, dw):
    pairs = []
    for x in range(N_X):
        for w in range(N_W):
            pairs.append((x * N_W + w, ((x + dx) % N_X) * N_W + (w + dw) % N_W))
    return lax.ppermute(array, "head", pairs)


WHOLE = pl.BlockSpec(memory_space=pltpu.VMEM)
IN_HBM = pl.BlockSpec(memory_space=pltpu.HBM)
ANYWHERE = pl.BlockSpec(memory_space=pl.ANY)


def rows_of(block):
    return pl.ds(pl.multiple_of(block * BLK, BLK), BLK)


def fetch_lists(vert_hbm, offs_hbm, vert, offs, sems):
    return (
        pltpu.make_async_copy(vert_hbm, vert, sems.at[0]),
        pltpu.make_async_copy(offs_hbm, offs, sems.at[1]),
    )


def gather_kernel(
    vert_hbm,
    offs_hbm,
    keys_ref,
    values_ref,
    fresh_keys_ref,
    fresh_values_ref,
    kv_ref,
    away_ref,
    next_ref,
    vert,
    offs,
    staged,
    list_sems,
    sems,
    slash_sems,
    next_sems,
):
    shard = lax.axis_index("ctx")
    away = 1 - (shard & 1)
    first = shard * LB
    lists = fetch_lists(vert_hbm, offs_hbm, vert, offs, list_sems)
    for copy in lists:
        copy.start()

    def vertical(i):
        block = vert[0, shard * VPB + i] - first
        return (
            pltpu.make_async_copy(
                values_ref.at[rows_of(block)], staged.at[i], sems.at[2 * i]
            ),
            pltpu.make_async_copy(
                keys_ref.at[rows_of(block)], kv_ref.at[pl.ds(i * BLK, BLK)], sems.at[2 * i + 1]
            ),
        )

    def slash(n):
        lower, upper = (NB + 2 * (n // 2) + away - offs[0, n % 2 + late] for late in (0, 2))
        block = jnp.where((lower >> 6) == shard, lower, upper)
        usable = ((block >> 6) == shard) & (vert[0, block >> 2] != block)
        local_rows = rows_of(block & (LB - 1))
        pair = (
            pltpu.make_async_copy(
                keys_ref.at[local_rows], away_ref.at[pl.ds(n * BLK, BLK)], slash_sems.at[2 * n]
            ),
            pltpu.make_async_copy(
                values_ref.at[local_rows],
                away_ref.at[pl.ds((SLOTS + n) * BLK, BLK)],
                slash_sems.at[2 * n + 1],
            ),
        )
        return usable, pair

    def following(keys, values):
        return (
            pltpu.make_async_copy(keys, next_ref.at[pl.ds(0, BLK)], next_sems.at[0]),
            pltpu.make_async_copy(values, next_ref.at[pl.ds(BLK, BLK)], next_sems.at[1]),
        )

    tail = pl.ds((LB - 1) * BLK, BLK)
    last = shard == N_Y * N_Z * N_K - 1
    from_cache = following(keys_ref.at[tail], values_ref.at[tail])
    from_fresh = following(fresh_keys_ref, fresh_values_ref)

    @pl.when(last)
    def _():
        for copy in from_cache:
            copy.start()

    @pl.when(jnp.logical_not(last))
    def _():
        for copy in from_fresh:
            copy.start()

    for copy in lists:
        copy.wait()
    for i in range(VPB):
        for copy in vertical(i):
            copy.start()

    holds_slash = (shard + 1) * LB > NB - SLASH_REACH

    @pl.when(holds_slash)
    def _():
        for n in range(SLOTS):
            usable, pair = slash(n)

            @pl.when(usable)
            def _(pair=pair):
                for copy in pair:
                    copy.start()

    for i in range(VPB):
        for copy in vertical(i):
            copy.wait()
        kv_ref[KEYS + i * BLK : KEYS + (i + 1) * BLK, :] = staged[i].T

    @pl.when(holds_slash)
    def _():
        for n in range(SLOTS):
            usable, pair = slash(n)

            @pl.when(usable)
            def _(pair=pair):
                for copy in pair:
                    copy.wait()

    @pl.when(last)
    def _():
        for copy in from_cache:
            copy.wait()

    @pl.when(jnp.logical_not(last))
    def _():
        for copy in from_fresh:
            copy.wait()


LISTS = [pltpu.SMEM((1, NV), jnp.int32), pltpu.SMEM((1, NS), jnp.int32)]


def gather_blocks(vertical_blocks, slash_offsets, keys, values, fresh_keys, fresh_values):
    return pl.pallas_call(
        gather_kernel,
        out_shape=[
            jax.ShapeDtypeStruct((2 * KEYS, DH), jnp.bfloat16),
            jax.ShapeDtypeStruct((2 * SLOTS * BLK, DH), jnp.bfloat16),
            jax.ShapeDtypeStruct((2 * BLK, DH), jnp.bfloat16),
        ],
        in_specs=[IN_HBM] * 6,
        out_specs=[WHOLE, IN_HBM, IN_HBM],
        scratch_shapes=LISTS
        + [
            pltpu.VMEM((VPB, BLK, DH), jnp.bfloat16),
            pltpu.SemaphoreType.DMA((2,)),
            pltpu.SemaphoreType.DMA((2 * VPB,)),
            pltpu.SemaphoreType.DMA((2 * SLOTS,)),
            pltpu.SemaphoreType.DMA((2,)),
        ],
        compiler_params=pltpu.CompilerParams(vmem_limit_bytes=8 * 2**20),
        cost_estimate=pl.CostEstimate(flops=0, bytes_accessed=12 * 2**20, transcendentals=0),
        name="gather_blocks",
    )(vertical_blocks, slash_offsets, keys, values, fresh_keys, fresh_values)


def attend_kernel(kind, dy, dz, piece, *refs):
    vert_hbm, offs_hbm, q_ref, keys_ref, values_ref = refs[:5]
    refs = refs[5:]
    if kind == FIRST:
        (own_ref, fresh_keys_ref, fresh_values_ref), refs = refs[:3], refs[3:]
        held_refs = (own_ref,)
    elif kind == LAST_HALF:
        (peer_ref, theirs_ref, near_ref), refs = refs[:3], refs[3:]
        held_refs = (peer_ref,)
    else:
        (own_ref, peer_ref, theirs_ref), refs = refs[:3], refs[3:]
        held_refs = (own_ref, peer_ref)
    if kind != FIRST:
        out_weight_ref, refs = refs[0], refs[1:]
        (out_ref, piece_ref, piece_sem), refs = (refs[0], refs[1], refs[-1]), (refs[0], *refs[2:-1])
        piece_copy = pltpu.make_async_copy(
            out_weight_ref.at[:, pl.ds(piece * TILE, TILE)], piece_ref, piece_sem.at[0]
        )
    out_ref, vert, offs, total, peak, weight, slash_keys, slash_values, list_sems, sems = refs[:10]
    rows = q_ref.shape[0]
    shard = lax.axis_index("ctx")
    query_block = (((shard >> 2) - dy) & (N_Y - 1)) * (N_Z * N_K) + ((shard & 3) ^ (N_K * dz))
    lists = fetch_lists(vert_hbm, offs_hbm, vert, offs, list_sems)
    for copy in lists:
        copy.start()

    def slash(j):
        block = NB + query_block - offs[0, j]
        fresh = vert[0, block >> 2] != block
        slot = (query_block >> 1) * 2 + (j & 1)
        holder = block >> 6

        def pair(own):
            if own:
                at = rows_of(block & (LB - 1))
                sources = keys_ref.at[at], values_ref.at[at]
            else:
                sources = theirs_ref.at[rows_of(slot)], theirs_ref.at[rows_of(SLOTS + slot)]
            return (
                pltpu.make_async_copy(sources[0], slash_keys.at[rows_of(j % PLACES)], sems.at[2 * j]),
                pltpu.make_async_copy(
                    sources[1], slash_values.at[rows_of(j % PLACES)], sems.at[2 * j + 1]
                ),
            )

        return fresh & (holder == shard), fresh & (holder == (shard ^ 1)), pair

    def scores(keys, allowed=None):
        s = lax.dot_general(keys, q_ref[...], LAST, preferred_element_type=jnp.float32) * SCALE
        return s if allowed is None else jnp.where(allowed, s, NEGATIVE)

    def weigh(values, p):
        width = values.shape[1]
        marked = jnp.concatenate([values, jnp.ones((STATS, width), jnp.bfloat16)], axis=0)
        return jnp.dot(marked, p.astype(jnp.bfloat16), preferred_element_type=jnp.float32)

    def begin():
        total[...] = jnp.zeros_like(total)
        peak[0:1, :] = jnp.max(scores(held_refs[0][:BLK, :]), axis=0, keepdims=True)
        weight[0:1, :] = jnp.zeros((1, rows), jnp.float32)

    def quick(keys, values, allowed=None):
        added = weigh(values, jnp.exp2(scores(keys, allowed) - peak[0:1, :]))
        weight[0:1, :] += added[DH : DH + 1]
        total[...] += added[:DH]

    def careful(keys, values, allowed=None):
        s = scores(keys, allowed)
        before = peak[0:1, :]
        now = jnp.maximum(before, jnp.max(s, axis=0, keepdims=True))
        shrink = jnp.exp2(before - now)
        added = weigh(values, jnp.exp2(s - now))
        weight[0:1, :] = weight[0:1, :] * shrink + added[DH : DH + 1]
        total[...] = total[...] * shrink + added[:DH]
        peak[0:1, :] = now

    def few(take):
        if kind == FIRST:
            key_at = lax.broadcasted_iota(jnp.int32, (BLK, rows), 0)
            token = lax.broadcasted_iota(jnp.int32, (BLK, rows), 1) >> 3
            take(fresh_keys_ref[...], fresh_values_ref[...].T, key_at <= token)
        elif kind == LAST_HALF:
            last_repeated = vert[0, NV - 1] == NB - 1

            @pl.when(jnp.logical_not((query_block == 0) & last_repeated))
            def _():
                take(near_ref[:BLK, :], near_ref[BLK:, :].T)

    def many(ref):
        values = jnp.concatenate(
            [ref[KEYS + i * BLK : KEYS + (i + 1) * BLK, :] for i in range(VPB)], axis=1
        )
        quick(ref[:KEYS, :], values)

    def holding():
        return [is_mine | is_theirs for is_mine, is_theirs, _ in map(slash, range(NS))]

    def start_slash():
        for j in range(NS):
            is_mine, is_theirs, pair = slash(j)
            for own, flag in ((True, is_mine), (False, is_theirs)):

                @pl.when(flag)
                def _(pair=pair, own=own):
                    for copy in pair(own):
                        copy.start()

    def take_slash():
        held = holding()

        @pl.when(held[0] | held[1] | held[2] | held[3])
        def _():
            taken = [held[0] | held[3], held[1], held[2]]
            for j in range(NS):

                @pl.when(held[j])
                def _(j=j):
                    for copy in slash(j)[2](True):
                        copy.wait()

            for place in range(PLACES):

                @pl.when(jnp.logical_not(taken[place]))
                def _(place=place):
                    at = slice(place * BLK, (place + 1) * BLK)
                    slash_keys[at, :] = jnp.zeros((BLK, DH), jnp.bfloat16)
                    slash_values[at, :] = jnp.zeros((BLK, DH), jnp.bfloat16)

            place_at = lax.broadcasted_iota(jnp.int32, (PLACES * BLK, rows), 0) // BLK
            bits = [jnp.where(flag, 1 << place, 0) for place, flag in enumerate(taken)]
            allowed = (((bits[0] + bits[1] + bits[2]) >> place_at) & 1) == 1
            quick(slash_keys[...], slash_values[...].T, allowed)

    if kind != FIRST:
        piece_copy.start()
    begin()
    if kind != LAST_HALF:
        many(own_ref)
    for copy in lists:
        copy.wait()
    if kind != FIRST:
        start_slash()
        many(peer_ref)
        take_slash()
    few(quick)
    outside = jnp.max(jnp.where(weight[0:1, :] < LIMIT, 0.0, 1.0))

    @pl.when(outside > 0.0)
    def _():
        begin()
        for ref in held_refs:

            def step(i, carry, ref=ref):
                at = pl.multiple_of(i * BLK, BLK)
                careful(ref[pl.ds(at, BLK), :], ref[pl.ds(KEYS + at, BLK), :])
                return carry

            lax.fori_loop(0, VPB, step, 0)

        for j, flag in enumerate(() if kind == FIRST else holding()):

            @pl.when(flag)
            def _(j=j):
                at = slice((j % PLACES) * BLK, (j % PLACES + 1) * BLK)
                careful(slash_keys[at, :], slash_values[at, :].T)

        few(careful)

    weights = weight[0:1, :]
    result = total[...] * (1.0 / weights)
    level = peak[0:1, :] + jnp.log2(weights)
    if kind != FAR:
        out_ref[:DH, :] = result
        out_ref[DH:, :] = jnp.broadcast_to(level, (8, rows))
    else:
        out_ref[:DH, :] = result.astype(jnp.bfloat16)
        high = level.astype(jnp.bfloat16).astype(jnp.float32)
        middle = (level - high).astype(jnp.bfloat16).astype(jnp.float32)
        low = level - high - middle
        line = lax.broadcasted_iota(jnp.int32, (STATS, rows), 0)
        stats = jnp.where(line == 0, high, jnp.where(line == 1, middle, jnp.where(line == 2, low, 0.0)))
        out_ref[DH:, :] = stats.astype(jnp.bfloat16)
    if kind != FIRST:
        piece_copy.wait()


def attend(kind, lists, q, cache, *operands, dy=0, dz=0, piece=0):
    rows = q.shape[0]
    if kind == FAR:
        shape = jax.ShapeDtypeStruct((DH + STATS, rows), jnp.bfloat16)
    else:
        shape = jax.ShapeDtypeStruct((DH + 8, rows), jnp.float32)
    specs = {
        FAR: [WHOLE, WHOLE, ANYWHERE, IN_HBM],
        FIRST: [WHOLE, WHOLE, WHOLE],
        LAST_HALF: [WHOLE, ANYWHERE, WHOLE, IN_HBM],
    }[kind]
    shapes = [shape]
    if kind != FIRST:
        shapes.append(jax.ShapeDtypeStruct((GROUP * DH, TILE), jnp.bfloat16))
    shards = 2 if kind == FAR else 1
    return pl.pallas_call(
        functools.partial(attend_kernel, kind, dy, dz, piece),
        out_shape=shapes,
        in_specs=[IN_HBM] * 2 + [WHOLE] + [IN_HBM] * 2 + specs,
        out_specs=[WHOLE] * len(shapes),
        scratch_shapes=LISTS
        + [
            pltpu.VMEM((DH, rows), jnp.float32),
            pltpu.VMEM((8, rows), jnp.float32),
            pltpu.VMEM((8, rows), jnp.float32),
            pltpu.VMEM((PLACES * BLK, DH), jnp.bfloat16),
            pltpu.VMEM((PLACES * BLK, DH), jnp.bfloat16),
            pltpu.SemaphoreType.DMA((2,)),
            pltpu.SemaphoreType.DMA((2 * NS,)),
            pltpu.SemaphoreType.DMA((1,)),
        ],
        compiler_params=pltpu.CompilerParams(vmem_limit_bytes=VMEM_BYTES),
        cost_estimate=pl.CostEstimate(
            flops=shards * KEYS * rows * DH * 10,
            bytes_accessed=shards * 2**21,
            transcendentals=shards * KEYS * rows,
        ),
        name=f"{kind}_{dy}{dz}" if kind == FAR else kind,
    )(*lists, q, *cache, *operands)


def project_kernel(first_ref, last_ref, *refs):
    count = N_Y * N_Z - 1
    part_refs, piece_refs = refs[:count], refs[count : count + HEADS]
    out_refs, (upright, natural, rotated) = refs[count + HEADS : -3], refs[-3:]
    levels = [first_ref[DH : DH + 1, :], last_ref[DH : DH + 1, :]]
    for ref in part_refs:
        stats = ref[DH:, :].astype(jnp.float32)
        levels.append(stats[0:1] + stats[1:2] + stats[2:3])
    highest = functools.reduce(jnp.maximum, levels)
    factors = [jnp.exp2(level - highest) for level in levels]
    blended = 0.0
    for ref, factor in zip((first_ref, last_ref, *part_refs), factors):
        blended += ref[:DH, :].astype(jnp.float32) * factor
    blended = blended * (1.0 / sum(factors))
    upright[...] = blended.T
    for h in range(GROUP):
        natural[:, h * DH : (h + 1) * DH] = upright[
            pl.ds(h, BLK, stride=GROUP), :
        ].astype(jnp.bfloat16)
    place = lax.axis_index("head")
    x, w = place >> 1, place & 1
    for at in range(HEADS):
        target = ((x + at // N_W) & (N_X - 1)) * N_W + ((w + at) & 1)
        rotated[at * SHARE : (at + 1) * SHARE, :] = natural[
            pl.ds(pl.multiple_of(target * SHARE, SHARE), SHARE), :
        ]
    for i, piece_ref in enumerate(piece_refs):
        column = i * TILE
        partial = jnp.dot(
            rotated[...], piece_ref[...], preferred_element_type=jnp.float32
        ).astype(jnp.bfloat16)
        for at in range(HEADS):
            out_refs[at][:, column : column + TILE] = partial[at * SHARE : (at + 1) * SHARE, :]


def project(halves, parts, pieces):
    depth, width = pieces[0].shape[0], TILE * len(pieces)
    return pl.pallas_call(
        project_kernel,
        out_shape=[jax.ShapeDtypeStruct((SHARE, width), jnp.bfloat16)] * HEADS,
        in_specs=[WHOLE] * (2 + len(parts) + len(pieces)),
        out_specs=[WHOLE] * HEADS,
        scratch_shapes=[
            pltpu.VMEM((ROWS, DH), jnp.float32),
            pltpu.VMEM((BLK, depth), jnp.bfloat16),
            pltpu.VMEM((BLK, depth), jnp.bfloat16),
        ],
        compiler_params=pltpu.CompilerParams(vmem_limit_bytes=12 * 2**20),
        cost_estimate=pl.CostEstimate(
            flops=2 * BLK * depth * width, bytes_accessed=2 * depth * width, transcendentals=0
        ),
        name="project",
    )(*halves, *parts, *map(in_vmem, pieces))


def in_hbm(x):
    return pltpu.with_memory_space_constraint(x, pltpu.HBM)


def in_vmem(x):
    return pltpu.with_memory_space_constraint(x, pltpu.VMEM)


def after(x, *earlier):
    return lax.optimization_barrier((x, *earlier))[0]


def local(
    queries,
    cache_keys,
    cache_values,
    new_keys,
    new_values,
    vertical_blocks,
    slash_offsets,
    out_weight,
):
    keys = in_hbm(cache_keys.reshape(-1, DH))
    values = in_hbm(cache_values.reshape(-1, DH))
    fresh_keys = new_keys.reshape(BLK, DH)
    fresh_values = new_values.reshape(BLK, DH)
    q = queries.reshape(ROWS, DH)
    held = {(0, 0): q, (0, 1): ctx_shift(q, 0, 1, 0)}
    for dy in (1, 3):
        held[dy, 0] = ctx_shift(q, dy, 0, 0)
    lists = (in_hbm(vertical_blocks), in_hbm(slash_offsets))
    kv, away, following = gather_blocks(
        lists[0],
        lists[1],
        keys,
        values,
        in_hbm(fresh_keys),
        in_hbm(fresh_values),
    )
    peer = ctx_shift(kv, 0, 0, 1)
    theirs = ctx_shift(away, 0, 0, 1)
    kv, peer, cache = in_vmem(kv), in_vmem(peer), (keys, values)
    (first,) = attend(FIRST, lists, in_vmem(q), cache, kv, fresh_keys, fresh_values)
    out_weight = in_hbm(out_weight)
    results, parts, weights = [first], [], []
    for dy, dz in ((0, 1), (3, 0), (1, 1), (3, 1), (2, 1), (2, 0), (1, 0)):
        if len(results) == 1:
            held[dy, dz] = after(held[dy, dz], held[1, 0], held[3, 0])
            for shift in (1, 3):
                held[shift, 1] = ctx_shift(after(held[0, 1], first), shift, 0, 0)
        elif len(results) == 2:
            for z in range(N_Z):
                held[2, z] = ctx_shift(after(held[0, z], results[1]), 2, 0, 0)
            near = lax.ppermute(
                after(following, results[1]), "ctx", [(i, (i + 1) % 16) for i in range(16)]
            )
        elif len(results) == 4:
            held[dy, dz] = after(held[dy, dz], near)
        rows = after(held[dy, dz], results[-1], *parts[: max(0, len(parts) - LAG)])
        result, weight = attend(
            FAR,
            lists,
            in_vmem(rows),
            cache,
            kv,
            peer,
            theirs,
            out_weight,
            dy=dy,
            dz=dz,
            piece=len(weights),
        )
        results.append(result)
        weights.append(weight)
        parts.append(ctx_shift(result, -dy, dz, 0))
    rows = after(q, results[-1], *parts[: len(parts) - LAG])
    last, weight = attend(
        LAST_HALF, lists, in_vmem(rows), cache, peer, theirs, near, out_weight, piece=len(weights)
    )
    pieces = project((first, last), parts, [*weights, weight])
    summed = pieces[0].astype(jnp.float32)
    received = []
    for at in range(1, HEADS):
        received.append(head_shift(pieces[at], at // N_W, at % N_W))
    for piece in received:
        summed = summed + piece.astype(jnp.float32)
    return summed.astype(jnp.bfloat16)


def solution(mesh):
    in_specs = (
        P("ctx", "head", None),
        P("ctx", "head", None),
        P("ctx", "head", None),
        P("ctx", "head", None),
        P("ctx", "head", None),
        P("head", None),
        P("head", None),
        P("head", None),
    )
    out_specs = P(("ctx", "head"), None)
    return jax.shard_map(local, mesh=mesh, in_specs=in_specs, out_specs=out_specs, check_vma=False)
```

```python
import functools
import math

import jax
import jax.numpy as jnp
from jax import lax
from jax.experimental import pallas as pl
from jax.experimental.pallas import tpu as pltpu
from jax.sharding import PartitionSpec as P

BLK = 128
DH = 128
GROUP = 8
ROWS = BLK * GROUP
LB = 64
VPB = 16
NS = 4
NB = 1024
N_Y = 4
N_Z = 2
N_K = 2
N_X = 4
N_W = 2
QB = 16
PAR = QB // N_K
KEYS = VPB * BLK
STATS = 16
SLOTS = 2 * PAR
SLASH_REACH = 271
NV = NB // 4
HEADS = N_X * N_W
SHARE = BLK // HEADS
TILE = 1024
LAG = 3
FAR = "far"
FIRST = "home_first"
LAST_HALF = "home_last"
PLACES = 3
SCALE = DH**-0.5 * math.log2(math.e)
NEGATIVE = -1e30
LIMIT = 1e30
VMEM_BYTES = 24 * 2**20
LAST = (((1,), (1,)), ((), ()))


def ctx_shift(x, dy, dz, dk):
    pairs = []
    for y in range(N_Y):
        for z in range(N_Z):
            for k in range(N_K):
                source = (y * N_Z + z) * N_K + k
                target = (((y + dy) % N_Y) * N_Z + (z + dz) % N_Z) * N_K + (k + dk) % N_K
                pairs.append((source, target))
    return lax.ppermute(x, "ctx", pairs)


def head_shift(array, dx, dw):
    pairs = []
    for x in range(N_X):
        for w in range(N_W):
            pairs.append((x * N_W + w, ((x + dx) % N_X) * N_W + (w + dw) % N_W))
    return lax.ppermute(array, "head", pairs)


WHOLE = pl.BlockSpec(memory_space=pltpu.VMEM)
IN_HBM = pl.BlockSpec(memory_space=pltpu.HBM)
ANYWHERE = pl.BlockSpec(memory_space=pl.ANY)


def rows_of(block):
    return pl.ds(pl.multiple_of(block * BLK, BLK), BLK)


def fetch_lists(vert_hbm, offs_hbm, vert, offs, sems):
    return (
        pltpu.make_async_copy(vert_hbm, vert, sems.at[0]),
        pltpu.make_async_copy(offs_hbm, offs, sems.at[1]),
    )


def gather_kernel(
    vert_hbm,
    offs_hbm,
    keys_ref,
    values_ref,
    fresh_keys_ref,
    fresh_values_ref,
    kv_ref,
    away_ref,
    next_ref,
    vert,
    offs,
    staged,
    list_sems,
    sems,
    slash_sems,
    next_sems,
):
    shard = lax.axis_index("ctx")
    away = 1 - (shard & 1)
    first = shard * LB
    lists = fetch_lists(vert_hbm, offs_hbm, vert, offs, list_sems)
    for copy in lists:
        copy.start()

    def vertical(i):
        block = vert[0, shard * VPB + i] - first
        return (
            pltpu.make_async_copy(
                values_ref.at[rows_of(block)], staged.at[i], sems.at[2 * i]
            ),
            pltpu.make_async_copy(
                keys_ref.at[rows_of(block)], kv_ref.at[pl.ds(i * BLK, BLK)], sems.at[2 * i + 1]
            ),
        )

    def slash(n):
        lower, upper = (NB + 2 * (n // 2) + away - offs[0, n % 2 + late] for late in (0, 2))
        block = jnp.where((lower >> 6) == shard, lower, upper)
        usable = ((block >> 6) == shard) & (vert[0, block >> 2] != block)
        local_rows = rows_of(block & (LB - 1))
        pair = (
            pltpu.make_async_copy(
                keys_ref.at[local_rows], away_ref.at[pl.ds(n * BLK, BLK)], slash_sems.at[2 * n]
            ),
            pltpu.make_async_copy(
                values_ref.at[local_rows],
                away_ref.at[pl.ds((SLOTS + n) * BLK, BLK)],
                slash_sems.at[2 * n + 1],
            ),
        )
        return usable, pair

    def following(keys, values):
        return (
            pltpu.make_async_copy(keys, next_ref.at[pl.ds(0, BLK)], next_sems.at[0]),
            pltpu.make_async_copy(values, next_ref.at[pl.ds(BLK, BLK)], next_sems.at[1]),
        )

    tail = pl.ds((LB - 1) * BLK, BLK)
    last = shard == N_Y * N_Z * N_K - 1
    from_cache = following(keys_ref.at[tail], values_ref.at[tail])
    from_fresh = following(fresh_keys_ref, fresh_values_ref)

    @pl.when(last)
    def _():
        for copy in from_cache:
            copy.start()

    @pl.when(jnp.logical_not(last))
    def _():
        for copy in from_fresh:
            copy.start()

    for copy in lists:
        copy.wait()
    for i in range(VPB):
        for copy in vertical(i):
            copy.start()

    holds_slash = (shard + 1) * LB > NB - SLASH_REACH

    @pl.when(holds_slash)
    def _():
        for n in range(SLOTS):
            usable, pair = slash(n)

            @pl.when(usable)
            def _(pair=pair):
                for copy in pair:
                    copy.start()

    for i in range(VPB):
        for copy in vertical(i):
            copy.wait()
        kv_ref[KEYS + i * BLK : KEYS + (i + 1) * BLK, :] = staged[i].T

    @pl.when(holds_slash)
    def _():
        for n in range(SLOTS):
            usable, pair = slash(n)

            @pl.when(usable)
            def _(pair=pair):
                for copy in pair:
                    copy.wait()

    @pl.when(last)
    def _():
        for copy in from_cache:
            copy.wait()

    @pl.when(jnp.logical_not(last))
    def _():
        for copy in from_fresh:
            copy.wait()


LISTS = [pltpu.SMEM((1, NV), jnp.int32), pltpu.SMEM((1, NS), jnp.int32)]


def gather_blocks(vertical_blocks, slash_offsets, keys, values, fresh_keys, fresh_values):
    return pl.pallas_call(
        gather_kernel,
        out_shape=[
            jax.ShapeDtypeStruct((2 * KEYS, DH), jnp.bfloat16),
            jax.ShapeDtypeStruct((2 * SLOTS * BLK, DH), jnp.bfloat16),
            jax.ShapeDtypeStruct((2 * BLK, DH), jnp.bfloat16),
        ],
        in_specs=[IN_HBM] * 6,
        out_specs=[WHOLE, IN_HBM, IN_HBM],
        scratch_shapes=LISTS
        + [
            pltpu.VMEM((VPB, BLK, DH), jnp.bfloat16),
            pltpu.SemaphoreType.DMA((2,)),
            pltpu.SemaphoreType.DMA((2 * VPB,)),
            pltpu.SemaphoreType.DMA((2 * SLOTS,)),
            pltpu.SemaphoreType.DMA((2,)),
        ],
        compiler_params=pltpu.CompilerParams(vmem_limit_bytes=8 * 2**20),
        cost_estimate=pl.CostEstimate(flops=0, bytes_accessed=12 * 2**20, transcendentals=0),
        name="gather_blocks",
    )(vertical_blocks, slash_offsets, keys, values, fresh_keys, fresh_values)


def attend_kernel(kind, dy, dz, piece, *refs):
    vert_hbm, offs_hbm, q_ref, keys_ref, values_ref = refs[:5]
    refs = refs[5:]
    if kind == FIRST:
        (own_ref, fresh_keys_ref, fresh_values_ref), refs = refs[:3], refs[3:]
        held_refs = (own_ref,)
    elif kind == LAST_HALF:
        (peer_ref, theirs_ref, near_ref), refs = refs[:3], refs[3:]
        held_refs = (peer_ref,)
    else:
        (own_ref, peer_ref, theirs_ref), refs = refs[:3], refs[3:]
        held_refs = (own_ref, peer_ref)
    if kind != FIRST:
        out_weight_ref, refs = refs[0], refs[1:]
        (out_ref, piece_ref, piece_sem), refs = (refs[0], refs[1], refs[-1]), (refs[0], *refs[2:-1])
        piece_copy = pltpu.make_async_copy(
            out_weight_ref.at[:, pl.ds(piece * TILE, TILE)], piece_ref, piece_sem.at[0]
        )
    out_ref, vert, offs, total, peak, weight, slash_keys, slash_values, list_sems, sems = refs[:10]
    rows = q_ref.shape[0]
    shard = lax.axis_index("ctx")
    query_block = (((shard >> 2) - dy) & (N_Y - 1)) * (N_Z * N_K) + ((shard & 3) ^ (N_K * dz))
    lists = fetch_lists(vert_hbm, offs_hbm, vert, offs, list_sems)
    for copy in lists:
        copy.start()

    def slash(j):
        block = NB + query_block - offs[0, j]
        fresh = vert[0, block >> 2] != block
        slot = (query_block >> 1) * 2 + (j & 1)
        holder = block >> 6

        def pair(own):
            if own:
                at = rows_of(block & (LB - 1))
                sources = keys_ref.at[at], values_ref.at[at]
            else:
                sources = theirs_ref.at[rows_of(slot)], theirs_ref.at[rows_of(SLOTS + slot)]
            return (
                pltpu.make_async_copy(sources[0], slash_keys.at[rows_of(j % PLACES)], sems.at[2 * j]),
                pltpu.make_async_copy(
                    sources[1], slash_values.at[rows_of(j % PLACES)], sems.at[2 * j + 1]
                ),
            )

        return fresh & (holder == shard), fresh & (holder == (shard ^ 1)), pair

    def scores(keys, allowed=None):
        s = lax.dot_general(keys, q_ref[...], LAST, preferred_element_type=jnp.float32) * SCALE
        return s if allowed is None else jnp.where(allowed, s, NEGATIVE)

    def weigh(values, p):
        width = values.shape[1]
        marked = jnp.concatenate([values, jnp.ones((STATS, width), jnp.bfloat16)], axis=0)
        return jnp.dot(marked, p.astype(jnp.bfloat16), preferred_element_type=jnp.float32)

    def begin():
        total[...] = jnp.zeros_like(total)
        peak[0:1, :] = jnp.max(scores(held_refs[0][:BLK, :]), axis=0, keepdims=True)
        weight[0:1, :] = jnp.zeros((1, rows), jnp.float32)

    def quick(keys, values, allowed=None):
        added = weigh(values, jnp.exp2(scores(keys, allowed) - peak[0:1, :]))
        weight[0:1, :] += added[DH : DH + 1]
        total[...] += added[:DH]

    def careful(keys, values, allowed=None):
        s = scores(keys, allowed)
        before = peak[0:1, :]
        now = jnp.maximum(before, jnp.max(s, axis=0, keepdims=True))
        shrink = jnp.exp2(before - now)
        added = weigh(values, jnp.exp2(s - now))
        weight[0:1, :] = weight[0:1, :] * shrink + added[DH : DH + 1]
        total[...] = total[...] * shrink + added[:DH]
        peak[0:1, :] = now

    def few(take):
        if kind == FIRST:
            key_at = lax.broadcasted_iota(jnp.int32, (BLK, rows), 0)
            token = lax.broadcasted_iota(jnp.int32, (BLK, rows), 1) >> 3
            take(fresh_keys_ref[...], fresh_values_ref[...].T, key_at <= token)
        elif kind == LAST_HALF:
            last_repeated = vert[0, NV - 1] == NB - 1

            @pl.when(jnp.logical_not((query_block == 0) & last_repeated))
            def _():
                take(near_ref[:BLK, :], near_ref[BLK:, :].T)

    def many(ref):
        values = jnp.concatenate(
            [ref[KEYS + i * BLK : KEYS + (i + 1) * BLK, :] for i in range(VPB)], axis=1
        )
        quick(ref[:KEYS, :], values)

    def holding():
        return [is_mine | is_theirs for is_mine, is_theirs, _ in map(slash, range(NS))]

    def start_slash():
        for j in range(NS):
            is_mine, is_theirs, pair = slash(j)
            for own, flag in ((True, is_mine), (False, is_theirs)):

                @pl.when(flag)
                def _(pair=pair, own=own):
                    for copy in pair(own):
                        copy.start()

    def take_slash():
        held = holding()

        @pl.when(held[0] | held[1] | held[2] | held[3])
        def _():
            taken = [held[0] | held[3], held[1], held[2]]
            for j in range(NS):

                @pl.when(held[j])
                def _(j=j):
                    for copy in slash(j)[2](True):
                        copy.wait()

            for place in range(PLACES):

                @pl.when(jnp.logical_not(taken[place]))
                def _(place=place):
                    at = slice(place * BLK, (place + 1) * BLK)
                    slash_keys[at, :] = jnp.zeros((BLK, DH), jnp.bfloat16)
                    slash_values[at, :] = jnp.zeros((BLK, DH), jnp.bfloat16)

            place_at = lax.broadcasted_iota(jnp.int32, (PLACES * BLK, rows), 0) // BLK
            bits = [jnp.where(flag, 1 << place, 0) for place, flag in enumerate(taken)]
            allowed = (((bits[0] + bits[1] + bits[2]) >> place_at) & 1) == 1
            quick(slash_keys[...], slash_values[...].T, allowed)

    if kind != FIRST:
        piece_copy.start()
    begin()
    if kind != LAST_HALF:
        many(own_ref)
    for copy in lists:
        copy.wait()
    if kind != FIRST:
        start_slash()
        many(peer_ref)
        take_slash()
    few(quick)
    outside = jnp.max(jnp.where(weight[0:1, :] < LIMIT, 0.0, 1.0))

    @pl.when(outside > 0.0)
    def _():
        begin()
        for ref in held_refs:

            def step(i, carry, ref=ref):
                at = pl.multiple_of(i * BLK, BLK)
                careful(ref[pl.ds(at, BLK), :], ref[pl.ds(KEYS + at, BLK), :])
                return carry

            lax.fori_loop(0, VPB, step, 0)

        for j, flag in enumerate(() if kind == FIRST else holding()):

            @pl.when(flag)
            def _(j=j):
                at = slice((j % PLACES) * BLK, (j % PLACES + 1) * BLK)
                careful(slash_keys[at, :], slash_values[at, :].T)

        few(careful)

    weights = weight[0:1, :]
    result = total[...] * (1.0 / weights)
    level = peak[0:1, :] + jnp.log2(weights)
    if kind != FAR:
        out_ref[:DH, :] = result
        out_ref[DH:, :] = jnp.broadcast_to(level, (8, rows))
    else:
        out_ref[:DH, :] = result.astype(jnp.bfloat16)
        high = level.astype(jnp.bfloat16).astype(jnp.float32)
        middle = (level - high).astype(jnp.bfloat16).astype(jnp.float32)
        low = level - high - middle
        line = lax.broadcasted_iota(jnp.int32, (STATS, rows), 0)
        stats = jnp.where(line == 0, high, jnp.where(line == 1, middle, jnp.where(line == 2, low, 0.0)))
        out_ref[DH:, :] = stats.astype(jnp.bfloat16)
    if kind != FIRST:
        piece_copy.wait()


def attend(kind, lists, q, cache, *operands, dy=0, dz=0, piece=0):
    rows = q.shape[0]
    if kind == FAR:
        shape = jax.ShapeDtypeStruct((DH + STATS, rows), jnp.bfloat16)
    else:
        shape = jax.ShapeDtypeStruct((DH + 8, rows), jnp.float32)
    specs = {
        FAR: [WHOLE, WHOLE, ANYWHERE, IN_HBM],
        FIRST: [WHOLE, WHOLE, WHOLE],
        LAST_HALF: [WHOLE, ANYWHERE, WHOLE, IN_HBM],
    }[kind]
    shapes = [shape]
    if kind != FIRST:
        shapes.append(jax.ShapeDtypeStruct((GROUP * DH, TILE), jnp.bfloat16))
    shards = 2 if kind == FAR else 1
    return pl.pallas_call(
        functools.partial(attend_kernel, kind, dy, dz, piece),
        out_shape=shapes,
        in_specs=[IN_HBM] * 2 + [WHOLE] + [IN_HBM] * 2 + specs,
        out_specs=[WHOLE] * len(shapes),
        scratch_shapes=LISTS
        + [
            pltpu.VMEM((DH, rows), jnp.float32),
            pltpu.VMEM((8, rows), jnp.float32),
            pltpu.VMEM((8, rows), jnp.float32),
            pltpu.VMEM((PLACES * BLK, DH), jnp.bfloat16),
            pltpu.VMEM((PLACES * BLK, DH), jnp.bfloat16),
            pltpu.SemaphoreType.DMA((2,)),
            pltpu.SemaphoreType.DMA((2 * NS,)),
            pltpu.SemaphoreType.DMA((1,)),
        ],
        compiler_params=pltpu.CompilerParams(vmem_limit_bytes=VMEM_BYTES),
        cost_estimate=pl.CostEstimate(
            flops=shards * KEYS * rows * DH * 10,
            bytes_accessed=shards * 2**21,
            transcendentals=shards * KEYS * rows,
        ),
        name=f"{kind}_{dy}{dz}" if kind == FAR else kind,
    )(*lists, q, *cache, *operands)


def project_kernel(first_ref, last_ref, *refs):
    count = N_Y * N_Z - 1
    part_refs, piece_refs = refs[:count], refs[count : count + HEADS]
    out_refs, (upright, natural, rotated) = refs[count + HEADS : -3], refs[-3:]
    levels = [first_ref[DH : DH + 1, :], last_ref[DH : DH + 1, :]]
    for ref in part_refs:
        stats = ref[DH:, :].astype(jnp.float32)
        levels.append(stats[0:1] + stats[1:2] + stats[2:3])
    highest = functools.reduce(jnp.maximum, levels)
    factors = [jnp.exp2(level - highest) for level in levels]
    blended = 0.0
    for ref, factor in zip((first_ref, last_ref, *part_refs), factors):
        blended += ref[:DH, :].astype(jnp.float32) * factor
    blended = blended * (1.0 / sum(factors))
    upright[...] = blended.T
    for h in range(GROUP):
        natural[:, h * DH : (h + 1) * DH] = upright[
            pl.ds(h, BLK, stride=GROUP), :
        ].astype(jnp.bfloat16)
    place = lax.axis_index("head")
    x, w = place >> 1, place & 1
    for at in range(HEADS):
        target = ((x + at // N_W) & (N_X - 1)) * N_W + ((w + at) & 1)
        rotated[at * SHARE : (at + 1) * SHARE, :] = natural[
            pl.ds(pl.multiple_of(target * SHARE, SHARE), SHARE), :
        ]
    for i, piece_ref in enumerate(piece_refs):
        column = i * TILE
        partial = jnp.dot(
            rotated[...], piece_ref[...], preferred_element_type=jnp.float32
        ).astype(jnp.bfloat16)
        for at in range(HEADS):
            out_refs[at][:, column : column + TILE] = partial[at * SHARE : (at + 1) * SHARE, :]


def project(halves, parts, pieces):
    depth, width = pieces[0].shape[0], TILE * len(pieces)
    return pl.pallas_call(
        project_kernel,
        out_shape=[jax.ShapeDtypeStruct((SHARE, width), jnp.bfloat16)] * HEADS,
        in_specs=[WHOLE] * (2 + len(parts) + len(pieces)),
        out_specs=[WHOLE] * HEADS,
        scratch_shapes=[
            pltpu.VMEM((ROWS, DH), jnp.float32),
            pltpu.VMEM((BLK, depth), jnp.bfloat16),
            pltpu.VMEM((BLK, depth), jnp.bfloat16),
        ],
        compiler_params=pltpu.CompilerParams(vmem_limit_bytes=12 * 2**20),
        cost_estimate=pl.CostEstimate(
            flops=2 * BLK * depth * width, bytes_accessed=2 * depth * width, transcendentals=0
        ),
        name="project",
    )(*halves, *parts, *map(in_vmem, pieces))


def in_hbm(x):
    return pltpu.with_memory_space_constraint(x, pltpu.HBM)


def in_vmem(x):
    return pltpu.with_memory_space_constraint(x, pltpu.VMEM)


def after(x, *earlier):
    return lax.optimization_barrier((x, *earlier))[0]


def local(
    queries,
    cache_keys,
    cache_values,
    new_keys,
    new_values,
    vertical_blocks,
    slash_offsets,
    out_weight,
):
    keys = in_hbm(cache_keys.reshape(-1, DH))
    values = in_hbm(cache_values.reshape(-1, DH))
    fresh_keys = new_keys.reshape(BLK, DH)
    fresh_values = new_values.reshape(BLK, DH)
    q = queries.reshape(ROWS, DH)
    held = {(0, 0): q, (0, 1): ctx_shift(q, 0, 1, 0)}
    for dy in (1, 3):
        held[dy, 0] = ctx_shift(q, dy, 0, 0)
    lists = (in_hbm(vertical_blocks), in_hbm(slash_offsets))
    kv, away, following = gather_blocks(
        lists[0],
        lists[1],
        keys,
        values,
        in_hbm(fresh_keys),
        in_hbm(fresh_values),
    )
    peer = ctx_shift(kv, 0, 0, 1)
    theirs = ctx_shift(away, 0, 0, 1)
    kv, peer, cache = in_vmem(kv), in_vmem(peer), (keys, values)
    (first,) = attend(FIRST, lists, in_vmem(q), cache, kv, fresh_keys, fresh_values)
    out_weight = in_hbm(out_weight)
    results, parts, weights = [first], [], []
    for dy, dz in ((0, 1), (3, 0), (1, 1), (3, 1), (2, 1), (2, 0), (1, 0)):
        if len(results) == 1:
            held[dy, dz] = after(held[dy, dz], held[1, 0], held[3, 0])
            for shift in (1, 3):
                held[shift, 1] = ctx_shift(after(held[0, 1], first), shift, 0, 0)
        elif len(results) == 2:
            for z in range(N_Z):
                held[2, z] = ctx_shift(after(held[0, z], results[1]), 2, 0, 0)
            near = lax.ppermute(
                after(following, results[1]), "ctx", [(i, (i + 1) % 16) for i in range(16)]
            )
        elif len(results) == 4:
            held[dy, dz] = after(held[dy, dz], near)
        rows = after(held[dy, dz], results[-1], *parts[: max(0, len(parts) - LAG)])
        result, weight = attend(
            FAR,
            lists,
            in_vmem(rows),
            cache,
            kv,
            peer,
            theirs,
            out_weight,
            dy=dy,
            dz=dz,
            piece=len(weights),
        )
        results.append(result)
        weights.append(weight)
        parts.append(ctx_shift(result, -dy, dz, 0))
    rows = after(q, results[-1], *parts[: len(parts) - LAG])
    last, weight = attend(
        LAST_HALF, lists, in_vmem(rows), cache, peer, theirs, near, out_weight, piece=len(weights)
    )
    pieces = project((first, last), parts, [*weights, weight])
    summed = pieces[0].astype(jnp.float32)
    received = []
    for at in (5, 3, 7, 4, 1, 2, 6):
        received.append(head_shift(pieces[at], at // N_W, at % N_W))
    for piece in received:
        summed = summed + piece.astype(jnp.float32)
    return summed.astype(jnp.bfloat16)


def solution(mesh):
    in_specs = (
        P("ctx", "head", None),
        P("ctx", "head", None),
        P("ctx", "head", None),
        P("ctx", "head", None),
        P("ctx", "head", None),
        P("head", None),
        P("head", None),
        P("head", None),
    )
    out_specs = P(("ctx", "head"), None)
    return jax.shard_map(local, mesh=mesh, in_specs=in_specs, out_specs=out_specs, check_vma=False)
```

```python
import functools
import math

import jax
import jax.numpy as jnp
from jax import lax
from jax.experimental import pallas as pl
from jax.experimental.pallas import tpu as pltpu
from jax.sharding import PartitionSpec as P

BLK = 128
DH = 128
GROUP = 8
ROWS = BLK * GROUP
LB = 64
VPB = 16
NS = 4
NB = 1024
N_Y = 4
N_Z = 2
N_K = 2
N_X = 4
N_W = 2
QB = 16
PAR = QB // N_K
KEYS = VPB * BLK
STATS = 16
SLOTS = 2 * PAR
SLASH_REACH = 271
NV = NB // 4
HEADS = N_X * N_W
SHARE = BLK // HEADS
TILE = 1024
LAG = 3
FAR = "far"
FIRST = "home_first"
LAST_HALF = "home_last"
PLACES = 3
SCALE = DH**-0.5 * math.log2(math.e)
NEGATIVE = -1e30
LIMIT = 1e30
VMEM_BYTES = 24 * 2**20
LAST = (((1,), (1,)), ((), ()))


def ctx_shift(x, dy, dz, dk):
    pairs = []
    for y in range(N_Y):
        for z in range(N_Z):
            for k in range(N_K):
                source = (y * N_Z + z) * N_K + k
                target = (((y + dy) % N_Y) * N_Z + (z + dz) % N_Z) * N_K + (k + dk) % N_K
                pairs.append((source, target))
    return lax.ppermute(x, "ctx", pairs)


def head_shift(array, dx, dw):
    pairs = []
    for x in range(N_X):
        for w in range(N_W):
            pairs.append((x * N_W + w, ((x + dx) % N_X) * N_W + (w + dw) % N_W))
    return lax.ppermute(array, "head", pairs)


WHOLE = pl.BlockSpec(memory_space=pltpu.VMEM)
IN_HBM = pl.BlockSpec(memory_space=pltpu.HBM)
ANYWHERE = pl.BlockSpec(memory_space=pl.ANY)


def rows_of(block):
    return pl.ds(pl.multiple_of(block * BLK, BLK), BLK)


def fetch_lists(vert_hbm, offs_hbm, vert, offs, sems):
    return (
        pltpu.make_async_copy(vert_hbm, vert, sems.at[0]),
        pltpu.make_async_copy(offs_hbm, offs, sems.at[1]),
    )


def gather_kernel(
    vert_hbm,
    offs_hbm,
    keys_ref,
    values_ref,
    fresh_keys_ref,
    fresh_values_ref,
    kv_ref,
    away_ref,
    next_ref,
    vert,
    offs,
    staged,
    list_sems,
    sems,
    slash_sems,
    next_sems,
):
    shard = lax.axis_index("ctx")
    away = 1 - (shard & 1)
    first = shard * LB
    lists = fetch_lists(vert_hbm, offs_hbm, vert, offs, list_sems)
    for copy in lists:
        copy.start()

    def vertical(i):
        block = vert[0, shard * VPB + i] - first
        return (
            pltpu.make_async_copy(
                values_ref.at[rows_of(block)], staged.at[i], sems.at[2 * i]
            ),
            pltpu.make_async_copy(
                keys_ref.at[rows_of(block)], kv_ref.at[pl.ds(i * BLK, BLK)], sems.at[2 * i + 1]
            ),
        )

    def slash(n):
        lower, upper = (NB + 2 * (n // 2) + away - offs[0, n % 2 + late] for late in (0, 2))
        block = jnp.where((lower >> 6) == shard, lower, upper)
        usable = ((block >> 6) == shard) & (vert[0, block >> 2] != block)
        local_rows = rows_of(block & (LB - 1))
        pair = (
            pltpu.make_async_copy(
                keys_ref.at[local_rows], away_ref.at[pl.ds(n * BLK, BLK)], slash_sems.at[2 * n]
            ),
            pltpu.make_async_copy(
                values_ref.at[local_rows],
                away_ref.at[pl.ds((SLOTS + n) * BLK, BLK)],
                slash_sems.at[2 * n + 1],
            ),
        )
        return usable, pair

    def following(keys, values):
        return (
            pltpu.make_async_copy(keys, next_ref.at[pl.ds(0, BLK)], next_sems.at[0]),
            pltpu.make_async_copy(values, next_ref.at[pl.ds(BLK, BLK)], next_sems.at[1]),
        )

    tail = pl.ds((LB - 1) * BLK, BLK)
    last = shard == N_Y * N_Z * N_K - 1
    from_cache = following(keys_ref.at[tail], values_ref.at[tail])
    from_fresh = following(fresh_keys_ref, fresh_values_ref)

    @pl.when(last)
    def _():
        for copy in from_cache:
            copy.start()

    @pl.when(jnp.logical_not(last))
    def _():
        for copy in from_fresh:
            copy.start()

    for copy in lists:
        copy.wait()
    for i in range(VPB):
        for copy in vertical(i):
            copy.start()

    holds_slash = (shard + 1) * LB > NB - SLASH_REACH

    @pl.when(holds_slash)
    def _():
        for n in range(SLOTS):
            usable, pair = slash(n)

            @pl.when(usable)
            def _(pair=pair):
                for copy in pair:
                    copy.start()

    for i in range(VPB):
        for copy in vertical(i):
            copy.wait()
        kv_ref[KEYS + i * BLK : KEYS + (i + 1) * BLK, :] = staged[i].T

    @pl.when(holds_slash)
    def _():
        for n in range(SLOTS):
            usable, pair = slash(n)

            @pl.when(usable)
            def _(pair=pair):
                for copy in pair:
                    copy.wait()

    @pl.when(last)
    def _():
        for copy in from_cache:
            copy.wait()

    @pl.when(jnp.logical_not(last))
    def _():
        for copy in from_fresh:
            copy.wait()


LISTS = [pltpu.SMEM((1, NV), jnp.int32), pltpu.SMEM((1, NS), jnp.int32)]


def gather_blocks(vertical_blocks, slash_offsets, keys, values, fresh_keys, fresh_values):
    return pl.pallas_call(
        gather_kernel,
        out_shape=[
            jax.ShapeDtypeStruct((2 * KEYS, DH), jnp.bfloat16),
            jax.ShapeDtypeStruct((2 * SLOTS * BLK, DH), jnp.bfloat16),
            jax.ShapeDtypeStruct((2 * BLK, DH), jnp.bfloat16),
        ],
        in_specs=[IN_HBM] * 6,
        out_specs=[WHOLE, IN_HBM, IN_HBM],
        scratch_shapes=LISTS
        + [
            pltpu.VMEM((VPB, BLK, DH), jnp.bfloat16),
            pltpu.SemaphoreType.DMA((2,)),
            pltpu.SemaphoreType.DMA((2 * VPB,)),
            pltpu.SemaphoreType.DMA((2 * SLOTS,)),
            pltpu.SemaphoreType.DMA((2,)),
        ],
        compiler_params=pltpu.CompilerParams(vmem_limit_bytes=8 * 2**20),
        cost_estimate=pl.CostEstimate(flops=0, bytes_accessed=12 * 2**20, transcendentals=0),
        name="gather_blocks",
    )(vertical_blocks, slash_offsets, keys, values, fresh_keys, fresh_values)


def attend_kernel(kind, dy, dz, piece, *refs):
    vert_hbm, offs_hbm, q_ref, keys_ref, values_ref = refs[:5]
    refs = refs[5:]
    if kind == FIRST:
        (own_ref, fresh_keys_ref, fresh_values_ref), refs = refs[:3], refs[3:]
        held_refs = (own_ref,)
    elif kind == LAST_HALF:
        (peer_ref, theirs_ref, near_ref), refs = refs[:3], refs[3:]
        held_refs = (peer_ref,)
    else:
        (own_ref, peer_ref, theirs_ref), refs = refs[:3], refs[3:]
        held_refs = (own_ref, peer_ref)
    if kind != FIRST:
        out_weight_ref, refs = refs[0], refs[1:]
        (out_ref, piece_ref, piece_sem), refs = (refs[0], refs[1], refs[-1]), (refs[0], *refs[2:-1])
        piece_copy = pltpu.make_async_copy(
            out_weight_ref.at[:, pl.ds(piece * TILE, TILE)], piece_ref, piece_sem.at[0]
        )
    out_ref, vert, offs, total, peak, weight, slash_keys, slash_values, list_sems, sems = refs[:10]
    rows = q_ref.shape[0]
    shard = lax.axis_index("ctx")
    query_block = (((shard >> 2) - dy) & (N_Y - 1)) * (N_Z * N_K) + ((shard & 3) ^ (N_K * dz))
    lists = fetch_lists(vert_hbm, offs_hbm, vert, offs, list_sems)
    for copy in lists:
        copy.start()

    def slash(j):
        block = NB + query_block - offs[0, j]
        fresh = vert[0, block >> 2] != block
        slot = (query_block >> 1) * 2 + (j & 1)
        holder = block >> 6

        def pair(own):
            if own:
                at = rows_of(block & (LB - 1))
                sources = keys_ref.at[at], values_ref.at[at]
            else:
                sources = theirs_ref.at[rows_of(slot)], theirs_ref.at[rows_of(SLOTS + slot)]
            return (
                pltpu.make_async_copy(sources[0], slash_keys.at[rows_of(j % PLACES)], sems.at[2 * j]),
                pltpu.make_async_copy(
                    sources[1], slash_values.at[rows_of(j % PLACES)], sems.at[2 * j + 1]
                ),
            )

        return fresh & (holder == shard), fresh & (holder == (shard ^ 1)), pair

    def scores(keys, allowed=None):
        s = lax.dot_general(keys, q_ref[...], LAST, preferred_element_type=jnp.float32) * SCALE
        return s if allowed is None else jnp.where(allowed, s, NEGATIVE)

    def weigh(values, p):
        width = values.shape[1]
        marked = jnp.concatenate([values, jnp.ones((STATS, width), jnp.bfloat16)], axis=0)
        return jnp.dot(marked, p.astype(jnp.bfloat16), preferred_element_type=jnp.float32)

    def begin():
        total[...] = jnp.zeros_like(total)
        peak[0:1, :] = jnp.max(scores(held_refs[0][:STATS, :]), axis=0, keepdims=True)
        weight[0:1, :] = jnp.zeros((1, rows), jnp.float32)

    def quick(keys, values, allowed=None):
        added = weigh(values, jnp.exp2(scores(keys, allowed) - peak[0:1, :]))
        weight[0:1, :] += added[DH : DH + 1]
        total[...] += added[:DH]

    def careful(keys, values, allowed=None):
        s = scores(keys, allowed)
        before = peak[0:1, :]
        now = jnp.maximum(before, jnp.max(s, axis=0, keepdims=True))
        shrink = jnp.exp2(before - now)
        added = weigh(values, jnp.exp2(s - now))
        weight[0:1, :] = weight[0:1, :] * shrink + added[DH : DH + 1]
        total[...] = total[...] * shrink + added[:DH]
        peak[0:1, :] = now

    def few(take):
        if kind == FIRST:
            key_at = lax.broadcasted_iota(jnp.int32, (BLK, rows), 0)
            token = lax.broadcasted_iota(jnp.int32, (BLK, rows), 1) >> 3
            take(fresh_keys_ref[...], fresh_values_ref[...].T, key_at <= token)
        elif kind == LAST_HALF:
            last_repeated = vert[0, NV - 1] == NB - 1

            @pl.when(jnp.logical_not((query_block == 0) & last_repeated))
            def _():
                take(near_ref[:BLK, :], near_ref[BLK:, :].T)

    def many(ref):
        values = jnp.concatenate(
            [ref[KEYS + i * BLK : KEYS + (i + 1) * BLK, :] for i in range(VPB)], axis=1
        )
        quick(ref[:KEYS, :], values)

    def holding():
        return [is_mine | is_theirs for is_mine, is_theirs, _ in map(slash, range(NS))]

    def start_slash():
        for j in range(NS):
            is_mine, is_theirs, pair = slash(j)
            for own, flag in ((True, is_mine), (False, is_theirs)):

                @pl.when(flag)
                def _(pair=pair, own=own):
                    for copy in pair(own):
                        copy.start()

    def take_slash():
        held = holding()

        @pl.when(held[0] | held[1] | held[2] | held[3])
        def _():
            taken = [held[0] | held[3], held[1], held[2]]
            for j in range(NS):

                @pl.when(held[j])
                def _(j=j):
                    for copy in slash(j)[2](True):
                        copy.wait()

            for place in range(PLACES):

                @pl.when(jnp.logical_not(taken[place]))
                def _(place=place):
                    at = slice(place * BLK, (place + 1) * BLK)
                    slash_keys[at, :] = jnp.zeros((BLK, DH), jnp.bfloat16)
                    slash_values[at, :] = jnp.zeros((BLK, DH), jnp.bfloat16)

            place_at = lax.broadcasted_iota(jnp.int32, (PLACES * BLK, rows), 0) // BLK
            bits = [jnp.where(flag, 1 << place, 0) for place, flag in enumerate(taken)]
            allowed = (((bits[0] + bits[1] + bits[2]) >> place_at) & 1) == 1
            quick(slash_keys[...], slash_values[...].T, allowed)

    if kind != FIRST:
        piece_copy.start()
    begin()
    if kind != LAST_HALF:
        many(own_ref)
    for copy in lists:
        copy.wait()
    if kind != FIRST:
        start_slash()
        many(peer_ref)
        take_slash()
    few(quick)
    outside = jnp.max(jnp.where(weight[0:1, :] < LIMIT, 0.0, 1.0))

    @pl.when(outside > 0.0)
    def _():
        begin()
        for ref in held_refs:

            def step(i, carry, ref=ref):
                at = pl.multiple_of(i * BLK, BLK)
                careful(ref[pl.ds(at, BLK), :], ref[pl.ds(KEYS + at, BLK), :])
                return carry

            lax.fori_loop(0, VPB, step, 0)

        for j, flag in enumerate(() if kind == FIRST else holding()):

            @pl.when(flag)
            def _(j=j):
                at = slice((j % PLACES) * BLK, (j % PLACES + 1) * BLK)
                careful(slash_keys[at, :], slash_values[at, :].T)

        few(careful)

    weights = weight[0:1, :]
    result = total[...] * (1.0 / weights)
    level = peak[0:1, :] + jnp.log2(weights)
    if kind != FAR:
        out_ref[:DH, :] = result
        out_ref[DH:, :] = jnp.broadcast_to(level, (8, rows))
    else:
        out_ref[:DH, :] = result.astype(jnp.bfloat16)
        high = level.astype(jnp.bfloat16).astype(jnp.float32)
        middle = (level - high).astype(jnp.bfloat16).astype(jnp.float32)
        low = level - high - middle
        line = lax.broadcasted_iota(jnp.int32, (STATS, rows), 0)
        stats = jnp.where(line == 0, high, jnp.where(line == 1, middle, jnp.where(line == 2, low, 0.0)))
        out_ref[DH:, :] = stats.astype(jnp.bfloat16)
    if kind != FIRST:
        piece_copy.wait()


def attend(kind, lists, q, cache, *operands, dy=0, dz=0, piece=0):
    rows = q.shape[0]
    if kind == FAR:
        shape = jax.ShapeDtypeStruct((DH + STATS, rows), jnp.bfloat16)
    else:
        shape = jax.ShapeDtypeStruct((DH + 8, rows), jnp.float32)
    specs = {
        FAR: [WHOLE, WHOLE, ANYWHERE, IN_HBM],
        FIRST: [WHOLE, WHOLE, WHOLE],
        LAST_HALF: [WHOLE, ANYWHERE, WHOLE, IN_HBM],
    }[kind]
    shapes = [shape]
    if kind != FIRST:
        shapes.append(jax.ShapeDtypeStruct((GROUP * DH, TILE), jnp.bfloat16))
    shards = 2 if kind == FAR else 1
    return pl.pallas_call(
        functools.partial(attend_kernel, kind, dy, dz, piece),
        out_shape=shapes,
        in_specs=[IN_HBM] * 2 + [WHOLE] + [IN_HBM] * 2 + specs,
        out_specs=[WHOLE] * len(shapes),
        scratch_shapes=LISTS
        + [
            pltpu.VMEM((DH, rows), jnp.float32),
            pltpu.VMEM((8, rows), jnp.float32),
            pltpu.VMEM((8, rows), jnp.float32),
            pltpu.VMEM((PLACES * BLK, DH), jnp.bfloat16),
            pltpu.VMEM((PLACES * BLK, DH), jnp.bfloat16),
            pltpu.SemaphoreType.DMA((2,)),
            pltpu.SemaphoreType.DMA((2 * NS,)),
            pltpu.SemaphoreType.DMA((1,)),
        ],
        compiler_params=pltpu.CompilerParams(vmem_limit_bytes=VMEM_BYTES),
        cost_estimate=pl.CostEstimate(
            flops=shards * KEYS * rows * DH * 10,
            bytes_accessed=shards * 2**21,
            transcendentals=shards * KEYS * rows,
        ),
        name=f"{kind}_{dy}{dz}" if kind == FAR else kind,
    )(*lists, q, *cache, *operands)


def project_kernel(first_ref, last_ref, *refs):
    count = N_Y * N_Z - 1
    part_refs, piece_refs = refs[:count], refs[count : count + HEADS]
    out_refs, (upright, natural, rotated) = refs[count + HEADS : -3], refs[-3:]
    levels = [first_ref[DH : DH + 1, :], last_ref[DH : DH + 1, :]]
    for ref in part_refs:
        stats = ref[DH:, :].astype(jnp.float32)
        levels.append(stats[0:1] + stats[1:2] + stats[2:3])
    highest = functools.reduce(jnp.maximum, levels)
    factors = [jnp.exp2(level - highest) for level in levels]
    blended = 0.0
    for ref, factor in zip((first_ref, last_ref, *part_refs), factors):
        blended += ref[:DH, :].astype(jnp.float32) * factor
    blended = blended * (1.0 / sum(factors))
    upright[...] = blended.T
    for h in range(GROUP):
        natural[:, h * DH : (h + 1) * DH] = upright[
            pl.ds(h, BLK, stride=GROUP), :
        ].astype(jnp.bfloat16)
    place = lax.axis_index("head")
    x, w = place >> 1, place & 1
    for at in range(HEADS):
        target = ((x + at // N_W) & (N_X - 1)) * N_W + ((w + at) & 1)
        rotated[at * SHARE : (at + 1) * SHARE, :] = natural[
            pl.ds(pl.multiple_of(target * SHARE, SHARE), SHARE), :
        ]
    for i, piece_ref in enumerate(piece_refs):
        column = i * TILE
        partial = jnp.dot(
            rotated[...], piece_ref[...], preferred_element_type=jnp.float32
        ).astype(jnp.bfloat16)
        for at in range(HEADS):
            out_refs[at][:, column : column + TILE] = partial[at * SHARE : (at + 1) * SHARE, :]


def project(halves, parts, pieces):
    depth, width = pieces[0].shape[0], TILE * len(pieces)
    return pl.pallas_call(
        project_kernel,
        out_shape=[jax.ShapeDtypeStruct((SHARE, width), jnp.bfloat16)] * HEADS,
        in_specs=[WHOLE] * (2 + len(parts) + len(pieces)),
        out_specs=[WHOLE] * HEADS,
        scratch_shapes=[
            pltpu.VMEM((ROWS, DH), jnp.float32),
            pltpu.VMEM((BLK, depth), jnp.bfloat16),
            pltpu.VMEM((BLK, depth), jnp.bfloat16),
        ],
        compiler_params=pltpu.CompilerParams(vmem_limit_bytes=12 * 2**20),
        cost_estimate=pl.CostEstimate(
            flops=2 * BLK * depth * width, bytes_accessed=2 * depth * width, transcendentals=0
        ),
        name="project",
    )(*halves, *parts, *map(in_vmem, pieces))


def in_hbm(x):
    return pltpu.with_memory_space_constraint(x, pltpu.HBM)


def in_vmem(x):
    return pltpu.with_memory_space_constraint(x, pltpu.VMEM)


def after(x, *earlier):
    return lax.optimization_barrier((x, *earlier))[0]


def local(
    queries,
    cache_keys,
    cache_values,
    new_keys,
    new_values,
    vertical_blocks,
    slash_offsets,
    out_weight,
):
    keys = in_hbm(cache_keys.reshape(-1, DH))
    values = in_hbm(cache_values.reshape(-1, DH))
    fresh_keys = new_keys.reshape(BLK, DH)
    fresh_values = new_values.reshape(BLK, DH)
    q = queries.reshape(ROWS, DH)
    held = {(0, 0): q, (0, 1): ctx_shift(q, 0, 1, 0)}
    for dy in (1, 3):
        held[dy, 0] = ctx_shift(q, dy, 0, 0)
    lists = (in_hbm(vertical_blocks), in_hbm(slash_offsets))
    kv, away, following = gather_blocks(
        lists[0],
        lists[1],
        keys,
        values,
        in_hbm(fresh_keys),
        in_hbm(fresh_values),
    )
    peer = ctx_shift(kv, 0, 0, 1)
    theirs = ctx_shift(away, 0, 0, 1)
    kv, peer, cache = in_vmem(kv), in_vmem(peer), (keys, values)
    (first,) = attend(FIRST, lists, in_vmem(q), cache, kv, fresh_keys, fresh_values)
    out_weight = in_hbm(out_weight)
    results, parts, weights = [first], [], []
    for dy, dz in ((0, 1), (3, 0), (1, 1), (3, 1), (2, 1), (2, 0), (1, 0)):
        if len(results) == 1:
            held[dy, dz] = after(held[dy, dz], held[1, 0], held[3, 0])
            for shift in (1, 3):
                held[shift, 1] = ctx_shift(after(held[0, 1], first), shift, 0, 0)
        elif len(results) == 2:
            for z in range(N_Z):
                held[2, z] = ctx_shift(after(held[0, z], results[1]), 2, 0, 0)
            near = lax.ppermute(
                after(following, results[1]), "ctx", [(i, (i + 1) % 16) for i in range(16)]
            )
        elif len(results) == 4:
            held[dy, dz] = after(held[dy, dz], near)
        rows = after(held[dy, dz], results[-1], *parts[: max(0, len(parts) - LAG)])
        result, weight = attend(
            FAR,
            lists,
            in_vmem(rows),
            cache,
            kv,
            peer,
            theirs,
            out_weight,
            dy=dy,
            dz=dz,
            piece=len(weights),
        )
        results.append(result)
        weights.append(weight)
        parts.append(ctx_shift(result, -dy, dz, 0))
    rows = after(q, results[-1], *parts[: len(parts) - LAG])
    last, weight = attend(
        LAST_HALF, lists, in_vmem(rows), cache, peer, theirs, near, out_weight, piece=len(weights)
    )
    pieces = project((first, last), parts, [*weights, weight])
    summed = pieces[0].astype(jnp.float32)
    received = []
    for at in (5, 3, 7, 4, 1, 2, 6):
        received.append(head_shift(pieces[at], at // N_W, at % N_W))
    for piece in received:
        summed = summed + piece.astype(jnp.float32)
    return summed.astype(jnp.bfloat16)


def solution(mesh):
    in_specs = (
        P("ctx", "head", None),
        P("ctx", "head", None),
        P("ctx", "head", None),
        P("ctx", "head", None),
        P("ctx", "head", None),
        P("head", None),
        P("head", None),
        P("head", None),
    )
    out_specs = P(("ctx", "head"), None)
    return jax.shard_map(local, mesh=mesh, in_specs=in_specs, out_specs=out_specs, check_vma=False)
```
